128 devices in a mesh: mem: 8 (over z, core), patch: 16 (over x, y).
Axes of the slice: x: 4, y: 4, z: 4, core: 2. Of those that a mesh axis runs over, the one named last changes fastest.
Arguments:
- ensemble: bfloat16 [1024, 12, 16384], P(('mem', 'patch')), may hold values from -6 to 6
- obs_col: int32 [16384], replicated, may hold values from 0 to 16383, as said below
- obs_var: int32 [16384], replicated, may hold values from 0 to 11
- obs_value: float32 [16384], replicated, may hold values from -8 to 8
- obs_err: float32 [16384], replicated, may hold values from 0.5 to 2
- obs_count: int32 [128], replicated, may hold values from 32 to 128, as said below
- coarse_list: int32 [512, 128], P(('mem', 'patch')), may hold values from 0 to 383, as said below
- coarse_count: int32 [512], P(('mem', 'patch')), may hold values from 32 to 128, as said below
Outputs:
- analysis: bfloat16 [1024, 12, 16384], P(('mem', 'patch'))
The draws below stay inside these ranges and needn't reach their ends.
Inputs may be any that keep to these rules, and one draw needn't show every extreme that they name: `obs_col`: slot j lies in column block j // 128, so its column is between (j // 128) * 128 and that plus 128 - 1. `obs_count`: patches whose index is 0 mod 4 hold 128 observations, those 2 mod 4 hold 32, the others between 64 and 128. `coarse_list`: entries of one row are distinct window rows of the coarse point's patch, all of present observations. `coarse_count`: the first coarse point of every patch uses all 128 slots.
All inputs are finite; a program needn't handle non-finite values. Where the reference program divides by a largest or mean magnitude, that divisor is 1e-20 or more.
Results may differ from the reference program's by a relative error of at most 0.0017.
Values may be sent and summed in bfloat16 or wider, within the bound.
A program may use at most 192 MiB of HBM per device.

```python
import math
import jax
import jax.numpy as jnp
from jax import lax

K = 1024
F = 12
COL_DEV = 128
OBS_DEV = 128
P_SIZE = 128
NS_STEPS = 4
NCG = 4
NPATCHES = 128
NCOL = 16384
NOBS = 16384
NCOARSE = 512
N_MEM = 8
N_PATCH = 16


def patch_counts(key):
    drawn = jax.random.randint(key, (NPATCHES,), OBS_DEV // 2, OBS_DEV + 1, dtype=jnp.int32)
    phase = jnp.arange(NPATCHES, dtype=jnp.int32) % 4
    full = jnp.full((NPATCHES,), OBS_DEV, dtype=jnp.int32)
    sparse = jnp.full((NPATCHES,), OBS_DEV // 4, dtype=jnp.int32)
    return jnp.where(phase == 0, full, jnp.where(phase == 2, sparse, drawn)).astype(jnp.int32)


def draw_obs_count(key, part):
    counts = patch_counts(key)
    return counts


def draw_obs_col(key, part):
    key = jax.random.fold_in(key, 11)
    block_index = jnp.arange(NOBS, dtype=jnp.int32) // OBS_DEV
    return (block_index * COL_DEV + jax.random.randint(key, (NOBS,), 0, COL_DEV, dtype=jnp.int32)).astype(jnp.int32)


def draw_coarse_list(key, part):
    counts = patch_counts(key)
    key = jax.random.fold_in(key, 12)
    row_keys = jax.random.split(key, NCOARSE)
    window_slot = jnp.arange(3 * OBS_DEV, dtype=jnp.int32)
    patch_of = jnp.arange(NCOARSE, dtype=jnp.int32) // NCG

    def pick_row(row_key, patch_index):
        owner = (patch_index - 1 + window_slot // OBS_DEV) % NPATCHES
        present = window_slot % OBS_DEV < counts[owner]
        order = jax.random.permutation(row_key, 3 * OBS_DEV).astype(jnp.int32)
        score = jnp.where(present, order, order + 3 * OBS_DEV)
        return jnp.argsort(score)[:P_SIZE]
    return jax.vmap(pick_row)(row_keys, patch_of).astype(jnp.int32)


def draw_coarse_count(key, part):
    key = jax.random.fold_in(key, 13)
    drawn = jax.random.randint(key, (NCOARSE,), P_SIZE // 4, P_SIZE + 1, dtype=jnp.int32)
    first_point = jnp.arange(NCOARSE, dtype=jnp.int32) % NCG == 0
    return jnp.where(first_point, P_SIZE, drawn).astype(jnp.int32)


def with_ends(result, rng, least, top_value):
    extent = result.shape
    place = [jax.random.randint(jax.random.fold_in(rng, axis), (), 0, extent[axis]) for axis in range(len(extent))]
    result = result.at[tuple(place)].set(least)
    longest = extent.index(max(extent))
    place[longest] = (place[longest] + 1) % extent[longest]
    return result.at[tuple(place)].set(top_value)


def block_scale(rng, shape, shards, low, largest):
    loudness, own = 1.0, jax.random.fold_in(rng, 6)
    for position, parts in shards:
        heights = jnp.exp(jax.random.uniform(jax.random.fold_in(own, position), (parts,), jnp.float32, low / len(shards), largest / len(shards)))
        loudness = loudness * jnp.repeat(heights, shape[position] // parts).reshape([-1 if axis == position else 1 for axis in range(len(shape))])
    return loudness


def noise(stream_key, dims, deviation, limit, pieces=(), kind=jnp.bfloat16):
    level = block_scale(stream_key, dims, pieces, -0.22, 0.18) if pieces else 1.0
    values = jax.random.normal(stream_key, dims, jnp.float32) * deviation * level
    return jnp.minimum(jnp.maximum(values, -limit), limit).astype(kind)


def setup_inputs(seed: int = 0) -> dict:
    keys = jax.random.split(jax.random.key(seed), 9)
    ensemble = noise(keys[0], (K, F, NCOL), 1.0, 6.0, ((0, 128),))
    obs_col = draw_obs_col(jax.random.fold_in(keys[8], 71), 0)
    obs_var = with_ends(jax.random.randint(keys[2], (NOBS,), 0, F), jax.random.fold_in(keys[2], 1), 0, F - 1).astype(jnp.int32)
    obs_value = noise(keys[3], (NOBS,), 1.5, 8.0, (), jnp.float32)
    obs_err = jnp.clip(jnp.exp(jax.random.uniform(keys[4], (NOBS,), jnp.float32, math.log(0.5), math.log(2.0))), 0.5, 2.0)
    obs_count = draw_obs_count(jax.random.fold_in(keys[8], 71), 0)
    coarse_list = draw_coarse_list(jax.random.fold_in(keys[8], 71), 0)
    coarse_count = draw_coarse_count(jax.random.fold_in(keys[8], 71), 0)
    return dict(ensemble=ensemble, obs_col=obs_col, obs_var=obs_var, obs_value=obs_value, obs_err=obs_err, obs_count=obs_count, coarse_list=coarse_list, coarse_count=coarse_count)


def analyse(background, window_rows, values, errors, columns, present, lists, counts, first_column, total_columns):
    f32 = jnp.float32
    highest = lax.Precision.HIGHEST
    members, fields, col_count = background.shape
    blocks, slots = lists.shape
    group = col_count // blocks
    dof_ratio = members - 1.0
    row_mean = lax.optimization_barrier(jnp.mean(window_rows.astype(f32), axis=0))
    obs_pert = (window_rows.astype(f32) - row_mean[None, :]).astype(jnp.bfloat16)
    innov = values - row_mean
    field_mean = lax.optimization_barrier(jnp.mean(background.astype(f32), axis=0))
    field_pert = (background.astype(f32) - field_mean[None, :, :]).astype(jnp.bfloat16)
    live_slot = (jnp.arange(slots, dtype=jnp.int32)[None, :] < counts[:, None]) & present[lists]
    centre = (first_column + group * jnp.arange(blocks, dtype=jnp.int32)).astype(f32) + 0.5 * (group - 1)
    offset = columns[lists].astype(f32) - centre[:, None]
    offset = offset - total_columns * jnp.floor(offset / total_columns + 0.5)
    weight = jnp.where(live_slot, jnp.exp(-(offset / col_count) ** 2) / errors[lists], 0.0).astype(f32)
    flat_list = lists.reshape(-1)
    picked = obs_pert[:, flat_list].astype(f32)
    full_gram = lax.dot_general(picked, picked, (((0,), (0,)), ((), ())), precision=highest)
    block_ids = jnp.arange(blocks, dtype=jnp.int32)
    gram = full_gram.reshape(blocks, slots, blocks, slots)[block_ids, :, block_ids, :]
    identity = jnp.eye(slots, dtype=f32)
    bmat = identity + weight[:, :, None] * gram * weight[:, None, :] / dof_ratio
    scale = lax.optimization_barrier(jnp.max(lax.optimization_barrier(jnp.sum(jnp.abs(bmat), axis=2)), axis=1))
    ymat = bmat / scale[:, None, None]
    zmat = jnp.broadcast_to(identity, bmat.shape)
    for newton_step in range(NS_STEPS):
        tmat = 0.5 * (3.0 * identity - jnp.matmul(zmat, ymat, precision=highest))
        ymat = jnp.matmul(ymat, tmat, precision=highest)
        zmat = jnp.matmul(tmat, zmat, precision=highest)
    root = jnp.sqrt(scale)[:, None, None] * ymat
    stacked = jnp.concatenate([bmat, bmat + root], axis=0)
    lowers = jnp.linalg.cholesky(stacked)
    inv_lowers = jax.scipy.linalg.solve_triangular(lowers, jnp.broadcast_to(identity, stacked.shape), lower=True)
    inv_b = inv_lowers[:blocks]
    inv_hl = inv_lowers[blocks:]
    inverse_h = jnp.matmul(jnp.swapaxes(inv_hl, 1, 2), inv_hl, precision=highest)
    rhs = weight * innov[lists]
    half = jnp.einsum('gij,gj->gi', inv_b, rhs, precision=highest)
    mean_weight = jnp.einsum('gji,gj->gi', inv_b, half, precision=highest) / dof_ratio
    mix = -(weight[:, :, None] * inverse_h * weight[:, None, :]) / dof_ratio
    shift_flat = (weight * mean_weight).reshape(-1)
    wide = fields * col_count
    pert_flat = field_pert.reshape(members, wide).astype(f32)
    proj = lax.dot_general(picked, pert_flat, (((0,), (0,)), ((), ())), precision=highest)
    own = (jnp.arange(blocks * slots, dtype=jnp.int32) // slots)[:, None] == (jnp.arange(col_count, dtype=jnp.int32) // group)[None, :]
    masked = jnp.where(own[:, None, :], proj.reshape(blocks * slots, fields, col_count), 0.0).reshape(blocks * slots, wide)
    mean_term = jnp.dot(shift_flat, masked, precision=highest)
    eye_blocks = jnp.eye(blocks, dtype=f32)
    mix_full = (eye_blocks[:, None, :, None] * mix[:, :, None, :]).reshape(blocks * slots, blocks * slots)
    spread_term = lax.dot_general(mix_full, masked, (((0,), (0,)), ((), ())), precision=highest).astype(jnp.bfloat16)
    update = jnp.dot(picked, spread_term.astype(f32), precision=highest)
    total = background.reshape(members, wide).astype(f32) + mean_term[None, :] + update
    return total.astype(jnp.bfloat16).reshape(members, fields, col_count)

def reference(ensemble, obs_col, obs_var, obs_value, obs_err, obs_count, coarse_list, coarse_count):
    devices = N_MEM * N_PATCH
    total_columns = COL_DEV * devices
    window_slot = jnp.arange(3 * OBS_DEV, dtype=jnp.int32)

    def one_patch(device_index):
        background = lax.dynamic_slice_in_dim(ensemble, (device_index * COL_DEV).astype(jnp.int32), COL_DEV, 2)
        owner = ((device_index - 1 + window_slot // OBS_DEV) % devices).astype(jnp.int32)
        window_index = (owner * OBS_DEV + window_slot % OBS_DEV).astype(jnp.int32)
        present = window_slot % OBS_DEV < obs_count[owner]
        window_rows = ensemble[:, obs_var[window_index], obs_col[window_index]]
        lists = lax.dynamic_slice_in_dim(coarse_list, (device_index * NCG).astype(jnp.int32), NCG, 0)
        counts = lax.dynamic_slice_in_dim(coarse_count, (device_index * NCG).astype(jnp.int32), NCG, 0)
        return analyse(background, window_rows, obs_value[window_index], obs_err[window_index], obs_col[window_index], present, lists, counts, (device_index * COL_DEV).astype(jnp.int32), float(total_columns))
    stacked = lax.map(one_patch, jnp.arange(devices, dtype=jnp.int32))
    return stacked.transpose(1, 2, 0, 3).reshape(K, F, total_columns)
```

```python
import jax
import jax.numpy as jnp
from jax import lax
from jax.experimental import pallas as pl
from jax.experimental.pallas import tpu as pltpu
from jax.sharding import PartitionSpec as P

MESH = pl.DeviceIdType.MESH
NS_STEPS = 4
DEVICES = 128
PATCHES_Y = 16
SLOTS = 128
GROUPS = 4
GROUP_COLS = 32
COLS = 128
FIELDS = 12
LOCAL = 8
MEMBERS = 1024
WINDOW = 3 * SLOTS
STRIDE = 37
PAIR = 2
LOAD_PARTS = 4


def dot(a, b, dims, precision=None):
    return lax.dot_general(
        a, b, (dims, ((), ())), preferred_element_type=jnp.float32, precision=precision
    )


def iota(shape, dim):
    return lax.broadcasted_iota(jnp.int32, shape, dim)


def kernel(
    x_ref,
    col_ref,
    var_ref,
    value_ref,
    err_ref,
    count_ref,
    list_ref,
    list_count_ref,
    y_ref,
    xv,
    rows_out,
    rows_in,
    fields_in,
    fields_out,
    pert,
    picked,
    picked_t,
    onehot,
    weight_row,
    weight_col,
    system,
    mix3,
    shift,
    load_sem,
    rows_send,
    rows_recv,
    fields_send,
    fields_recv,
    back_send,
    back_recv,
    own_sem,
):
    f32, bf16 = jnp.float32, jnp.bfloat16
    highest = lax.Precision.HIGHEST
    mem = lax.axis_index("mem")
    patch = lax.axis_index("patch")
    me = mem * PATCHES_Y + patch
    dof = MEMBERS - 1.0

    def device(t):
        return (t >> 4, t & 15)

    def partner(i):
        return me ^ ((i * STRIDE) & (DEVICES - 1))

    def columns_of(t):
        return pl.ds(pl.multiple_of(t * COLS, COLS), COLS)

    width = DEVICES * COLS // LOAD_PARTS
    loads = []
    for part in range(LOAD_PARTS):
        span = pl.ds(part * width, width)
        load = pltpu.make_async_copy(x_ref.at[:, :, span], xv.at[:, :, span], load_sem.at[part])
        load.start()
        loads.append(load)
    barrier = pltpu.get_barrier_semaphore()

    def greet(i, carry):
        pl.semaphore_signal(barrier, inc=1, device_id=device(partner(i)), device_id_type=MESH)
        return carry

    lax.fori_loop(1, DEVICES, greet, 0)

    def extract(p, carry):
        col = col_ref[pl.ds(p, 1), :] - p * COLS
        var = var_ref[pl.ds(p, 1), :]
        hot = jnp.where(iota((COLS, SLOTS), 0) == col, 1.0, 0.0).astype(bf16)
        tile = xv[:, :, columns_of(p)].reshape(FIELDS * LOCAL, COLS)
        picks = dot(tile, hot, ((1,), (0,)))
        found = jnp.zeros((LOCAL, SLOTS), f32)
        for f in range(FIELDS):
            found = jnp.where(var == f, picks[f * LOCAL : (f + 1) * LOCAL, :], found)
        rows_out[p + 1] = found.astype(bf16)
        return carry

    share = DEVICES // LOAD_PARTS
    for part in range(LOAD_PARTS):
        loads[part].wait()
        lax.fori_loop(part * share, (part + 1) * share, extract, 0, unroll=2)
    rows_out[0] = rows_out[DEVICES]
    rows_out[DEVICES + 1] = rows_out[1]
    rows_in[:, me] = rows_out[pl.ds(me, 3)]
    fields_in[:, me] = xv[:, :, columns_of(me)]

    pl.semaphore_wait(barrier, DEVICES - 1)

    def send_rows(i, carry):
        t = partner(i)
        pltpu.make_async_remote_copy(
            src_ref=rows_out.at[pl.ds(t, 3)],
            dst_ref=rows_in.at[:, me],
            send_sem=rows_send,
            recv_sem=rows_recv,
            device_id=device(t),
            device_id_type=MESH,
        ).start()
        return carry

    lax.fori_loop(1, DEVICES, send_rows, 0)

    def send_fields(i, carry):
        t = partner(i)
        pltpu.make_async_remote_copy(
            src_ref=xv.at[:, :, columns_of(t)],
            dst_ref=fields_in.at[:, me],
            send_sem=fields_send,
            recv_sem=fields_recv,
            device_id=device(t),
            device_id_type=MESH,
        ).start()
        return carry

    lax.fori_loop(1, DEVICES, send_fields, 0)

    window = [lax.rem(me + DEVICES - 1 + w, DEVICES) for w in range(3)]
    lane = iota((1, SLOTS), 1)
    eye = iota((SLOTS, SLOTS), 0) == iota((SLOTS, SLOTS), 1)

    def window_row(ref):
        return jnp.concatenate([ref[pl.ds(q, 1), :] for q in window], axis=1)

    def as_column(row):
        return jnp.sum(jnp.where(eye, row, 0.0), axis=1, keepdims=True)

    present = jnp.concatenate(
        [jnp.where(lane < count_ref[q], 1.0, 0.0).astype(f32) for q in window], axis=1
    )
    values = window_row(value_ref)
    table = jnp.concatenate(
        [
            window_row(err_ref),
            window_row(col_ref).astype(f32),
            present,
            jnp.zeros((5, WINDOW), f32),
        ],
        axis=0,
    )
    for g in range(GROUPS):
        listed = list_ref[g : g + 1, :]
        hot = jnp.where(iota((WINDOW, SLOTS), 0) == listed, 1.0, 0.0).astype(f32)
        onehot[:, g * SLOTS : (g + 1) * SLOTS] = hot.astype(bf16)
        looked = dot(table, hot, ((1,), (0,)), highest)
        err, col, there = looked[0:1, :], looked[1:2, :], looked[2:3, :]
        centre = (me * COLS + g * GROUP_COLS).astype(f32) + 0.5 * (GROUP_COLS - 1)
        offset = col - centre
        total = float(DEVICES * COLS)
        offset = offset - total * jnp.floor(offset / total + 0.5)
        live = (lane < list_count_ref[g]) & (there > 0.5)
        weight = jnp.where(live, jnp.exp(-((offset / COLS) ** 2)) / err, 0.0)
        weight_row[g : g + 1, :] = weight
        weight_col[g] = jnp.broadcast_to(as_column(weight), (SLOTS, SLOTS))

    everyone = rows_in.at[:, pl.ds(0, DEVICES - 1)]
    pltpu.make_async_copy(everyone, everyone, rows_recv).wait()
    means = []
    for w in range(3):
        rows = rows_in[w].reshape(MEMBERS, SLOTS).astype(f32)
        mean = jnp.sum(rows, axis=0, keepdims=True) * (1.0 / MEMBERS)
        means.append(mean)
        pert[:, w * SLOTS : (w + 1) * SLOTS] = (rows - mean).astype(bf16)
    innov = values - jnp.concatenate(means, axis=1)
    innov8 = jnp.concatenate([innov, jnp.zeros((7, WINDOW), f32)], axis=0)
    for g in range(GROUPS):
        span = slice(g * SLOTS, (g + 1) * SLOTS)
        hot = onehot[:, span]
        chosen = dot(pert[...], hot, ((1,), (0,)))
        picked[:, span] = chosen.astype(bf16)
        picked_t[span, :] = jnp.transpose(chosen).astype(bf16)

    identity = jnp.where(eye, 1.0, 0.0).astype(f32)
    for g in range(GROUPS):
        span = slice(g * SLOTS, (g + 1) * SLOTS)
        gram = dot(picked_t[span, :], picked[:, span], ((1,), (0,)))
        bmat = identity + weight_col[g] * gram * weight_row[g : g + 1, :] / dof
        system[g] = bmat
    ymats, zmats, scales = [], [], []
    for g in range(GROUPS):
        bmat = system[g]
        sums = jnp.sum(jnp.abs(bmat), axis=1, keepdims=True)
        scale = jnp.max(sums, axis=0, keepdims=True)
        scales.append(scale)
        ymats.append(bmat / scale)
        zmats.append(None)
    for step in range(NS_STEPS):
        if step == 0:
            tmats = [0.5 * (3.0 * identity - y) for y in ymats]
        else:
            tmats = [
                0.5 * (3.0 * identity - dot(z, y, ((1,), (0,)), highest))
                for z, y in zip(zmats, ymats)
            ]
        ymats = [dot(y, t, ((1,), (0,)), highest) for y, t in zip(ymats, tmats)]
        if step == 0:
            zmats = tmats
        elif step < NS_STEPS - 1:
            zmats = [dot(t, z, ((1,), (0,)), highest) for t, z in zip(tmats, zmats)]
    for g in range(GROUPS):
        system[GROUPS + g] = system[g] + jnp.sqrt(scales[g]) * ymats[g]

    lanes = iota((SLOTS, SLOTS), 1)

    def sweep(k, carry):
        index = jnp.full((SLOTS, SLOTS), k, jnp.int32)
        here = lanes == k
        for j in range(2 * GROUPS):
            mat = system[j]
            row = jnp.broadcast_to(system[j, pl.ds(k, 1), :], (8, SLOTS))
            column = jnp.take_along_axis(mat, index, axis=1, mode="promise_in_bounds")
            pivot = jnp.take_along_axis(row, index[:8], axis=1, mode="promise_in_bounds")
            inverse = 1.0 / pivot
            scaled = jnp.where(here[:8], -inverse, row * inverse)
            system[j] = jnp.where(here, 0.0, mat) - column * scaled[:1]
            system[j, pl.ds(k, 1), :] = scaled[:1]
        return carry

    lax.fori_loop(0, SLOTS, sweep, 0)

    group_of = iota((SLOTS, COLS), 1) // GROUP_COLS
    shift_sel = jnp.zeros((SLOTS, COLS), f32)
    for g in range(GROUPS):
        span = slice(g * SLOTS, (g + 1) * SLOTS)
        hot = onehot[:, span].astype(f32)
        seen = dot(innov8, hot, ((1,), (0,)), highest)[0:1, :]
        row = weight_row[g : g + 1, :]
        solved = -jnp.sum(system[g] * (row * seen), axis=1, keepdims=True)
        shift_sel = jnp.where(group_of == g, weight_col[g] * solved / dof, shift_sel)
        mix = weight_col[g] * system[GROUPS + g] * row / dof
        high = mix.astype(bf16)
        low = (mix - high.astype(f32)).astype(bf16)
        mix3[span, 0:SLOTS] = high
        mix3[span, SLOTS : 2 * SLOTS] = high
        mix3[span, 2 * SLOTS : 3 * SLOTS] = low
    shift[...] = shift_sel

    everyone_in = fields_in.at[:, pl.ds(0, DEVICES - 1)]
    pltpu.make_async_copy(everyone_in, everyone_in, fields_recv).wait()

    def update(c, carry):
        first = c * PAIR
        chunk = pl.ds(first, PAIR)
        whole = [
            fields_in[first + j].reshape(MEMBERS, COLS).astype(f32) for j in range(PAIR)
        ]
        whole = jnp.concatenate(whole, axis=1)
        mean = jnp.sum(whole, axis=0, keepdims=True) * (1.0 / MEMBERS)
        field_pert = (whole - mean).astype(bf16)
        proj = dot(picked_t[...], field_pert, ((1,), (0,)))
        group = (iota((SLOTS, PAIR * COLS), 1) % COLS) // GROUP_COLS
        own = jnp.zeros((SLOTS, PAIR * COLS), f32)
        for g in range(GROUPS):
            own = jnp.where(group == g, proj[g * SLOTS : (g + 1) * SLOTS, :], own)
        both = jnp.concatenate([shift[...]] * PAIR, axis=1)
        mean_term = jnp.sum(both * own, axis=0, keepdims=True)
        high = own.astype(bf16)
        low = (own - high.astype(f32)).astype(bf16)
        split = jnp.concatenate([high, low, high], axis=0)
        spread = dot(mix3[...], split, ((1,), (0,)))
        spread = jnp.concatenate(
            [
                jnp.where(group == g, spread[g * SLOTS : (g + 1) * SLOTS, :], 0.0)
                for g in range(GROUPS)
            ],
            axis=0,
        ).astype(bf16)
        total = whole + mean_term + dot(picked[...], spread, ((1,), (0,)))
        for j in range(PAIR):
            part = total[:, j * COLS : (j + 1) * COLS].astype(bf16)
            fields_out[first + j] = part.reshape(DEVICES, LOCAL, COLS)

        def send_back(i, inner):
            t = partner(i)
            pltpu.make_async_remote_copy(
                src_ref=fields_out.at[chunk, t],
                dst_ref=y_ref.at[chunk, :, columns_of(me)],
                send_sem=back_send,
                recv_sem=back_recv,
                device_id=device(t),
                device_id_type=MESH,
            ).start()
            return inner

        lax.fori_loop(1, DEVICES, send_back, 0)
        return carry

    lax.fori_loop(0, FIELDS // PAIR, update, 0)
    mine = pltpu.make_async_copy(fields_out.at[:, me], y_ref.at[:, :, columns_of(me)], own_sem)
    mine.start()
    sent_rows = rows_in.at[:, pl.ds(0, DEVICES - 1)]
    pltpu.make_async_copy(sent_rows, sent_rows, rows_send).wait()
    pltpu.make_async_copy(everyone_in, everyone_in, fields_send).wait()
    everyone_out = fields_out.at[:, pl.ds(0, DEVICES - 1)]
    pltpu.make_async_copy(everyone_out, everyone_out, back_send).wait()
    pltpu.make_async_copy(everyone_out, everyone_out, back_recv).wait()
    mine.wait()


def shards(ensemble, obs_col, obs_var, obs_value, obs_err, obs_count, coarse_list, coarse_count):
    f32, bf16 = jnp.float32, jnp.bfloat16
    by_field = jnp.transpose(ensemble, (1, 0, 2))
    square = (DEVICES, SLOTS)
    vmem = pl.BlockSpec(memory_space=pltpu.VMEM)
    smem = pl.BlockSpec(memory_space=pltpu.SMEM)
    anywhere = pl.BlockSpec(memory_space=pl.ANY)
    blocks = (FIELDS, DEVICES, LOCAL, COLS)
    result = pl.pallas_call(
        kernel,
        out_shape=jax.ShapeDtypeStruct((FIELDS, LOCAL, DEVICES * COLS), bf16),
        in_specs=[anywhere, vmem, vmem, vmem, vmem, smem, vmem, smem],
        out_specs=anywhere,
        scratch_shapes=[
            pltpu.VMEM((FIELDS, LOCAL, DEVICES * COLS), bf16),
            pltpu.VMEM((DEVICES + 2, LOCAL, SLOTS), bf16),
            pltpu.VMEM((3, DEVICES, LOCAL, SLOTS), bf16),
            pltpu.VMEM(blocks, bf16),
            pltpu.VMEM(blocks, bf16),
            pltpu.VMEM((MEMBERS, WINDOW), bf16),
            pltpu.VMEM((MEMBERS, GROUPS * SLOTS), bf16),
            pltpu.VMEM((GROUPS * SLOTS, MEMBERS), bf16),
            pltpu.VMEM((WINDOW, GROUPS * SLOTS), bf16),
            pltpu.VMEM((8, SLOTS), f32),
            pltpu.VMEM((GROUPS, SLOTS, SLOTS), f32),
            pltpu.VMEM((2 * GROUPS, SLOTS, SLOTS), f32),
            pltpu.VMEM((GROUPS * SLOTS, 3 * SLOTS), bf16),
            pltpu.VMEM((SLOTS, COLS), f32),
            pltpu.SemaphoreType.DMA((LOAD_PARTS,)),
        ]
        + [pltpu.SemaphoreType.DMA] * 7,
        compiler_params=pltpu.CompilerParams(
            collective_id=0, has_side_effects=True, vmem_limit_bytes=48 * 1024 * 1024
        ),
        cost_estimate=pl.CostEstimate(
            flops=6_000_000_000, bytes_accessed=12_000_000, transcendentals=1024
        ),
        name="letkf",
    )(
        by_field,
        obs_col.reshape(square),
        obs_var.reshape(square),
        obs_value.reshape(square),
        obs_err.reshape(square),
        obs_count,
        coarse_list,
        coarse_count,
    )
    return jnp.transpose(result, (1, 0, 2))


def solution(mesh):
    return jax.shard_map(
        shards,
        mesh=mesh,
        in_specs=(
            P(("mem", "patch"), None, None),
            P(),
            P(),
            P(),
            P(),
            P(),
            P(("mem", "patch"), None),
            P(("mem", "patch")),
        ),
        out_specs=P(("mem", "patch"), None, None),
        check_vma=False,
    )
```

```python
import jax
import jax.numpy as jnp
from jax import lax
from jax.experimental import pallas as pl
from jax.experimental.pallas import tpu as pltpu
from jax.sharding import PartitionSpec as P

MESH = pl.DeviceIdType.MESH
NS_STEPS = 4
DEVICES = 128
PATCHES_Y = 16
SLOTS = 128
GROUPS = 4
GROUP_COLS = 32
COLS = 128
FIELDS = 12
LOCAL = 8
MEMBERS = 1024
WINDOW = 3 * SLOTS
STRIDE = 37
PAIR = 2
LOAD_PARTS = 4
EARLY = 4
PANEL = 16


def dot(a, b, dims, precision=None):
    return lax.dot_general(
        a, b, (dims, ((), ())), preferred_element_type=jnp.float32, precision=precision
    )


def iota(shape, dim):
    return lax.broadcasted_iota(jnp.int32, shape, dim)


def kernel(
    x_ref,
    col_any,
    var_any,
    value_any,
    err_any,
    count_any,
    list_any,
    list_count_any,
    y_ref,
    col_ref,
    var_ref,
    value_ref,
    err_ref,
    count_ref,
    list_ref,
    list_count_ref,
    small_sem,
    xv,
    rows_out,
    rows_in,
    fields_in,
    fields_out,
    pert,
    picked,
    picked_t,
    onehot,
    weight_row,
    weight_col,
    system,
    mix3,
    shift,
    load_sem,
    rows_send,
    rows_recv,
    fields_send,
    fields_recv,
    back_send,
    back_recv,
    own_sem,
):
    f32, bf16 = jnp.float32, jnp.bfloat16
    highest = lax.Precision.HIGHEST
    mem = lax.axis_index("mem")
    patch = lax.axis_index("patch")
    me = mem * PATCHES_Y + patch
    dof = MEMBERS - 1.0

    def device(t):
        return (t >> 4, t & 15)

    def partner(i):
        return me ^ ((i * STRIDE) & (DEVICES - 1))

    def columns_of(t):
        return pl.ds(pl.multiple_of(t * COLS, COLS), COLS)

    small = []
    for k, (source, target) in enumerate(
        [
            (col_any, col_ref),
            (var_any, var_ref),
            (value_any, value_ref),
            (err_any, err_ref),
            (count_any, count_ref),
            (list_any, list_ref),
            (list_count_any, list_count_ref),
        ]
    ):
        load = pltpu.make_async_copy(source, target, small_sem.at[k])
        load.start()
        small.append(load)
    width = DEVICES * COLS // LOAD_PARTS
    loads = []
    for part in range(LOAD_PARTS):
        span = pl.ds(part * width, width)
        load = pltpu.make_async_copy(x_ref.at[:, :, span], xv.at[:, :, span], load_sem.at[part])
        load.start()
        loads.append(load)
    barrier = pltpu.get_barrier_semaphore()

    def greet(i, carry):
        pl.semaphore_signal(barrier, inc=1, device_id=device(partner(i)), device_id_type=MESH)
        return carry

    lax.fori_loop(1, DEVICES, greet, 0)

    pl.semaphore_wait(barrier, DEVICES - 1)

    def send_fields(first, count, part):
        span = pl.ds(first, count)

        def send(i, carry):
            t = partner(i)
            pltpu.make_async_remote_copy(
                src_ref=x_ref.at[span, :, columns_of(t)],
                dst_ref=fields_in.at[span, me],
                send_sem=fields_send.at[part],
                recv_sem=fields_recv.at[part],
                device_id=device(t),
                device_id_type=MESH,
            ).start()
            return carry

        lax.fori_loop(1, DEVICES, send, 0)

    send_fields(0, EARLY, 0)
    for load in small:
        load.wait()

    def extract(p, carry):
        col = col_ref[pl.ds(p, 1), :] - p * COLS
        var = var_ref[pl.ds(p, 1), :]
        hot = jnp.where(iota((COLS, SLOTS), 0) == col, 1.0, 0.0).astype(bf16)
        tile = xv[:, :, columns_of(p)].reshape(FIELDS * LOCAL, COLS)
        picks = dot(tile, hot, ((1,), (0,)))
        found = jnp.zeros((LOCAL, SLOTS), f32)
        for f in range(FIELDS):
            found = jnp.where(var == f, picks[f * LOCAL : (f + 1) * LOCAL, :], found)
        rows_out[p + 1] = found.astype(bf16)
        return carry

    share = DEVICES // LOAD_PARTS
    for part in range(LOAD_PARTS):
        loads[part].wait()
        lax.fori_loop(part * share, (part + 1) * share, extract, 0, unroll=2)
    rows_out[0] = rows_out[DEVICES]
    rows_out[DEVICES + 1] = rows_out[1]
    rows_in[:, me] = rows_out[pl.ds(me, 3)]
    fields_in[:, me] = xv[:, :, columns_of(me)]

    def send_rows(i, carry):
        t = partner(i)
        pltpu.make_async_remote_copy(
            src_ref=rows_out.at[pl.ds(t, 3)],
            dst_ref=rows_in.at[:, me],
            send_sem=rows_send,
            recv_sem=rows_recv,
            device_id=device(t),
            device_id_type=MESH,
        ).start()
        return carry

    lax.fori_loop(1, DEVICES, send_rows, 0)
    send_fields(EARLY, FIELDS - EARLY, 1)

    window = [lax.rem(me + DEVICES - 1 + w, DEVICES) for w in range(3)]
    lane = iota((1, SLOTS), 1)
    eye = iota((SLOTS, SLOTS), 0) == iota((SLOTS, SLOTS), 1)

    def window_row(ref):
        return jnp.concatenate([ref[pl.ds(q, 1), :] for q in window], axis=1)

    def as_column(row):
        return jnp.sum(jnp.where(eye, row, 0.0), axis=1, keepdims=True)

    present = jnp.concatenate(
        [jnp.where(lane < count_ref[q], 1.0, 0.0).astype(f32) for q in window], axis=1
    )
    values = window_row(value_ref)
    table = jnp.concatenate(
        [
            window_row(err_ref),
            window_row(col_ref).astype(f32),
            present,
            jnp.zeros((5, WINDOW), f32),
        ],
        axis=0,
    )
    for g in range(GROUPS):
        listed = list_ref[g : g + 1, :]
        hot = jnp.where(iota((WINDOW, SLOTS), 0) == listed, 1.0, 0.0).astype(f32)
        onehot[:, g * SLOTS : (g + 1) * SLOTS] = hot.astype(bf16)
        looked = dot(table, hot, ((1,), (0,)), highest)
        err, col, there = looked[0:1, :], looked[1:2, :], looked[2:3, :]
        centre = (me * COLS + g * GROUP_COLS).astype(f32) + 0.5 * (GROUP_COLS - 1)
        offset = col - centre
        total = float(DEVICES * COLS)
        offset = offset - total * jnp.floor(offset / total + 0.5)
        live = (lane < list_count_ref[g]) & (there > 0.5)
        weight = jnp.where(live, jnp.exp(-((offset / COLS) ** 2)) / err, 0.0)
        weight_row[g : g + 1, :] = weight
        weight_col[g] = jnp.broadcast_to(as_column(weight), (SLOTS, SLOTS))

    everyone = rows_in.at[:, pl.ds(0, DEVICES - 1)]
    pltpu.make_async_copy(everyone, everyone, rows_recv).wait()
    means = []
    for w in range(3):
        rows = rows_in[w].reshape(MEMBERS, SLOTS).astype(f32)
        mean = jnp.sum(rows, axis=0, keepdims=True) * (1.0 / MEMBERS)
        means.append(mean)
        pert[:, w * SLOTS : (w + 1) * SLOTS] = (rows - mean).astype(bf16)
    innov = values - jnp.concatenate(means, axis=1)
    innov8 = jnp.concatenate([innov, jnp.zeros((7, WINDOW), f32)], axis=0)
    for g in range(GROUPS):
        span = slice(g * SLOTS, (g + 1) * SLOTS)
        hot = onehot[:, span]
        chosen = dot(pert[...], hot, ((1,), (0,)))
        picked[:, span] = chosen.astype(bf16)
        picked_t[span, :] = jnp.transpose(chosen).astype(bf16)

    identity = jnp.where(eye, 1.0, 0.0).astype(f32)
    for g in range(GROUPS):
        span = slice(g * SLOTS, (g + 1) * SLOTS)
        gram = dot(picked_t[span, :], picked[:, span], ((1,), (0,)))
        bmat = identity + weight_col[g] * gram * weight_row[g : g + 1, :] / dof
        system[g] = bmat
    ymats, zmats, scales = [], [], []
    for g in range(GROUPS):
        bmat = system[g]
        sums = jnp.sum(jnp.abs(bmat), axis=1, keepdims=True)
        scale = jnp.max(sums, axis=0, keepdims=True)
        scales.append(scale)
        ymats.append(bmat / scale)
        zmats.append(None)
    for step in range(NS_STEPS):
        if step == 0:
            tmats = [0.5 * (3.0 * identity - y) for y in ymats]
        else:
            tmats = [
                0.5 * (3.0 * identity - dot(z, y, ((1,), (0,)), highest))
                for z, y in zip(zmats, ymats)
            ]
        ymats = [dot(y, t, ((1,), (0,)), highest) for y, t in zip(ymats, tmats)]
        if step == 0:
            zmats = tmats
        elif step < NS_STEPS - 1:
            zmats = [dot(t, z, ((1,), (0,)), highest) for t, z in zip(tmats, zmats)]
    for g in range(GROUPS):
        system[GROUPS + g] = system[g] + jnp.sqrt(scales[g]) * ymats[g]

    panel_lane = iota((1, SLOTS), 1)
    panel_row = iota((PANEL, SLOTS), 0)
    lanes = iota((SLOTS, SLOTS), 1)

    def thirds(a):
        high = a.astype(bf16)
        rest = a - high.astype(f32)
        mid = rest.astype(bf16)
        return high, mid, (rest - mid.astype(f32)).astype(bf16)

    for b in range(SLOTS // PANEL):
        rows = slice(b * PANEL, (b + 1) * PANEL)
        before = [system[j, rows, :] for j in range(2 * GROUPS)]
        after = list(before)
        for i in range(PANEL):
            c = b * PANEL + i
            here = panel_lane == c
            for j in range(2 * GROUPS):
                now = after[j]
                column = jnp.broadcast_to(now[:, c : c + 1], (PANEL, SLOTS))
                inverse = 1.0 / column[i : i + 1, :]
                scaled = jnp.where(here, -inverse, now[i : i + 1, :] * inverse)
                swept = jnp.where(here, 0.0, now) - column * scaled
                after[j] = jnp.where(panel_row == i, scaled, swept)
        inside = (lanes >= b * PANEL) & (lanes < (b + 1) * PANEL)
        for j in range(2 * GROUPS):
            h, m, l = thirds(before[j])
            p, q, r = thirds(after[j])
            left = jnp.concatenate([h, h, h, m, m, l], axis=0)
            right = jnp.concatenate([p, q, r, p, q, p], axis=0)
            step = dot(left, right, ((0,), (0,)))
            system[j] = jnp.where(inside, 0.0, system[j]) - step
            system[j, rows, :] = after[j]

    group_of = iota((SLOTS, COLS), 1) // GROUP_COLS
    shift_sel = jnp.zeros((SLOTS, COLS), f32)
    for g in range(GROUPS):
        span = slice(g * SLOTS, (g + 1) * SLOTS)
        hot = onehot[:, span].astype(f32)
        seen = dot(innov8, hot, ((1,), (0,)), highest)[0:1, :]
        row = weight_row[g : g + 1, :]
        solved = -jnp.sum(system[g] * (row * seen), axis=1, keepdims=True)
        shift_sel = jnp.where(group_of == g, weight_col[g] * solved / dof, shift_sel)
        mix = weight_col[g] * system[GROUPS + g] * row / dof
        high = mix.astype(bf16)
        low = (mix - high.astype(f32)).astype(bf16)
        mix3[span, 0:SLOTS] = high
        mix3[span, SLOTS : 2 * SLOTS] = high
        mix3[span, 2 * SLOTS : 3 * SLOTS] = low
    shift[...] = shift_sel

    early_in = fields_in.at[pl.ds(0, EARLY), pl.ds(0, DEVICES - 1)]
    late_in = fields_in.at[pl.ds(EARLY, FIELDS - EARLY), pl.ds(0, DEVICES - 1)]
    pltpu.make_async_copy(early_in, early_in, fields_recv.at[0]).wait()

    def update(c, carry):
        first = c * PAIR
        chunk = pl.ds(first, PAIR)

        @pl.when(c == EARLY // PAIR)
        def _():
            pltpu.make_async_copy(late_in, late_in, fields_recv.at[1]).wait()

        whole = [
            fields_in[first + j].reshape(MEMBERS, COLS).astype(f32) for j in range(PAIR)
        ]
        whole = jnp.concatenate(whole, axis=1)
        mean = jnp.sum(whole, axis=0, keepdims=True) * (1.0 / MEMBERS)
        field_pert = (whole - mean).astype(bf16)
        proj = dot(picked_t[...], field_pert, ((1,), (0,)))
        group = (iota((SLOTS, PAIR * COLS), 1) % COLS) // GROUP_COLS
        own = jnp.zeros((SLOTS, PAIR * COLS), f32)
        for g in range(GROUPS):
            own = jnp.where(group == g, proj[g * SLOTS : (g + 1) * SLOTS, :], own)
        both = jnp.concatenate([shift[...]] * PAIR, axis=1)
        mean_term = jnp.sum(both * own, axis=0, keepdims=True)
        high = own.astype(bf16)
        low = (own - high.astype(f32)).astype(bf16)
        split = jnp.concatenate([high, low, high], axis=0)
        spread = dot(mix3[...], split, ((1,), (0,)))
        spread = jnp.concatenate(
            [
                jnp.where(group == g, spread[g * SLOTS : (g + 1) * SLOTS, :], 0.0)
                for g in range(GROUPS)
            ],
            axis=0,
        ).astype(bf16)
        total = whole + mean_term + dot(picked[...], spread, ((1,), (0,)))
        for j in range(PAIR):
            part = total[:, j * COLS : (j + 1) * COLS].astype(bf16)
            fields_out[first + j] = part.reshape(DEVICES, LOCAL, COLS)

        def send_back(i, inner):
            t = partner(i)
            pltpu.make_async_remote_copy(
                src_ref=fields_out.at[chunk, t],
                dst_ref=y_ref.at[chunk, :, columns_of(me)],
                send_sem=back_send,
                recv_sem=back_recv,
                device_id=device(t),
                device_id_type=MESH,
            ).start()
            return inner

        lax.fori_loop(1, DEVICES, send_back, 0)
        return carry

    lax.fori_loop(0, FIELDS // PAIR, update, 0)
    mine = pltpu.make_async_copy(fields_out.at[:, me], y_ref.at[:, :, columns_of(me)], own_sem)
    mine.start()
    sent_rows = rows_in.at[:, pl.ds(0, DEVICES - 1)]
    pltpu.make_async_copy(sent_rows, sent_rows, rows_send).wait()
    pltpu.make_async_copy(early_in, early_in, fields_send.at[0]).wait()
    pltpu.make_async_copy(late_in, late_in, fields_send.at[1]).wait()
    everyone_out = fields_out.at[:, pl.ds(0, DEVICES - 1)]
    pltpu.make_async_copy(everyone_out, everyone_out, back_send).wait()
    pltpu.make_async_copy(everyone_out, everyone_out, back_recv).wait()
    mine.wait()


def shards(ensemble, obs_col, obs_var, obs_value, obs_err, obs_count, coarse_list, coarse_count):
    f32, bf16 = jnp.float32, jnp.bfloat16
    by_field = jnp.transpose(ensemble, (1, 0, 2))
    square = (DEVICES, SLOTS)
    anywhere = pl.BlockSpec(memory_space=pl.ANY)
    blocks = (FIELDS, DEVICES, LOCAL, COLS)
    result = pl.pallas_call(
        kernel,
        out_shape=jax.ShapeDtypeStruct((FIELDS, LOCAL, DEVICES * COLS), bf16),
        in_specs=[anywhere] * 8,
        out_specs=anywhere,
        scratch_shapes=[
            pltpu.VMEM(square, jnp.int32),
            pltpu.VMEM(square, jnp.int32),
            pltpu.VMEM(square, f32),
            pltpu.VMEM(square, f32),
            pltpu.SMEM((DEVICES,), jnp.int32),
            pltpu.VMEM((GROUPS, SLOTS), jnp.int32),
            pltpu.SMEM((GROUPS,), jnp.int32),
            pltpu.SemaphoreType.DMA((7,)),
            pltpu.VMEM((FIELDS, LOCAL, DEVICES * COLS), bf16),
            pltpu.VMEM((DEVICES + 2, LOCAL, SLOTS), bf16),
            pltpu.VMEM((3, DEVICES, LOCAL, SLOTS), bf16),
            pltpu.VMEM(blocks, bf16),
            pltpu.VMEM(blocks, bf16),
            pltpu.VMEM((MEMBERS, WINDOW), bf16),
            pltpu.VMEM((MEMBERS, GROUPS * SLOTS), bf16),
            pltpu.VMEM((GROUPS * SLOTS, MEMBERS), bf16),
            pltpu.VMEM((WINDOW, GROUPS * SLOTS), bf16),
            pltpu.VMEM((8, SLOTS), f32),
            pltpu.VMEM((GROUPS, SLOTS, SLOTS), f32),
            pltpu.VMEM((2 * GROUPS, SLOTS, SLOTS), f32),
            pltpu.VMEM((GROUPS * SLOTS, 3 * SLOTS), bf16),
            pltpu.VMEM((SLOTS, COLS), f32),
            pltpu.SemaphoreType.DMA((LOAD_PARTS,)),
        ]
        + [pltpu.SemaphoreType.DMA] * 2
        + [pltpu.SemaphoreType.DMA((2,))] * 2
        + [pltpu.SemaphoreType.DMA] * 3,
        compiler_params=pltpu.CompilerParams(
            collective_id=0, has_side_effects=True, vmem_limit_bytes=56 * 1024 * 1024
        ),
        cost_estimate=pl.CostEstimate(
            flops=6_000_000_000, bytes_accessed=12_000_000, transcendentals=1024
        ),
        name="letkf",
    )(
        by_field,
        obs_col.reshape(square),
        obs_var.reshape(square),
        obs_value.reshape(square),
        obs_err.reshape(square),
        obs_count,
        coarse_list,
        coarse_count,
    )
    return jnp.transpose(result, (1, 0, 2))


def solution(mesh):
    return jax.shard_map(
        shards,
        mesh=mesh,
        in_specs=(
            P(("mem", "patch"), None, None),
            P(),
            P(),
            P(),
            P(),
            P(),
            P(("mem", "patch"), None),
            P(("mem", "patch")),
        ),
        out_specs=P(("mem", "patch"), None, None),
        check_vma=False,
    )
```

```python
import jax
import jax.numpy as jnp
from jax import lax
from jax.experimental import pallas as pl
from jax.experimental.pallas import tpu as pltpu
from jax.sharding import PartitionSpec as P

MESH = pl.DeviceIdType.MESH
NS_STEPS = 4
DEVICES = 128
PATCHES_Y = 16
SLOTS = 128
GROUPS = 4
GROUP_COLS = 32
COLS = 128
FIELDS = 12
LOCAL = 8
MEMBERS = 1024
WINDOW = 3 * SLOTS
STRIDE = 45
PAIR = 2
LOAD_PARTS = 4
EARLY = 4
MATES = 22
PANEL = 16


def dot(a, b, dims, precision=None):
    return lax.dot_general(
        a, b, (dims, ((), ())), preferred_element_type=jnp.float32, precision=precision
    )


def iota(shape, dim):
    return lax.broadcasted_iota(jnp.int32, shape, dim)


def kernel(
    x_ref,
    col_any,
    var_any,
    value_any,
    err_any,
    count_any,
    list_any,
    list_count_any,
    y_ref,
    col_ref,
    var_ref,
    value_ref,
    err_ref,
    count_ref,
    list_ref,
    list_count_ref,
    small_sem,
    xv,
    rows_out,
    rows_in,
    fields_in,
    fields_out,
    pert,
    picked,
    picked_t,
    onehot,
    weight_row,
    weight_col,
    system,
    mix3,
    shift,
    load_sem,
    rows_send,
    rows_recv,
    fields_send,
    fields_recv,
    back_send,
    back_recv,
    own_sem,
    ready,
):
    f32, bf16 = jnp.float32, jnp.bfloat16
    highest = lax.Precision.HIGHEST
    mem = lax.axis_index("mem")
    patch = lax.axis_index("patch")
    me = mem * PATCHES_Y + patch
    dof = MEMBERS - 1.0

    def device(t):
        return (t >> 4, t & 15)

    def partner(i):
        return me ^ ((i * STRIDE) & (DEVICES - 1))

    def columns_of(t):
        return pl.ds(pl.multiple_of(t * COLS, COLS), COLS)

    small = []
    for k, (source, target) in enumerate(
        [
            (col_any, col_ref),
            (var_any, var_ref),
            (value_any, value_ref),
            (err_any, err_ref),
            (count_any, count_ref),
            (list_any, list_ref),
            (list_count_any, list_count_ref),
        ]
    ):
        load = pltpu.make_async_copy(source, target, small_sem.at[k])
        load.start()
        small.append(load)
    width = DEVICES * COLS // LOAD_PARTS
    loads = []
    for part in range(LOAD_PARTS):
        span = pl.ds(part * width, width)
        load = pltpu.make_async_copy(x_ref.at[:, :, span], xv.at[:, :, span], load_sem.at[part])
        load.start()
        loads.append(load)
    barrier = pltpu.get_barrier_semaphore()

    def mate(i):
        return me ^ jnp.where(i < PATCHES_Y, i, (i - PATCHES_Y + 1) * PATCHES_Y)

    def greet(i, carry):
        pl.semaphore_signal(barrier, inc=1, device_id=device(mate(i)), device_id_type=MESH)
        return carry

    lax.fori_loop(1, MATES + 1, greet, 0)

    def send_fields(t, part):
        span = pl.ds(0, EARLY) if part == 0 else pl.ds(EARLY, FIELDS - EARLY)
        pltpu.make_async_remote_copy(
            src_ref=x_ref.at[span, :, columns_of(t)],
            dst_ref=fields_in.at[span, me],
            send_sem=fields_send.at[part],
            recv_sem=fields_recv.at[part],
            device_id=device(t),
            device_id_type=MESH,
        ).start()

    def send_mates(part):
        def send(i, carry):
            send_fields(me ^ ((i * 7) & (PATCHES_Y - 1)), part)

            @pl.when(i < 8)
            def _():
                send_fields(me ^ (i * PATCHES_Y), part)

            return carry

        lax.fori_loop(1, PATCHES_Y, send, 0)

    def send_others(part):
        def send(i, carry):
            k = (i * STRIDE) & (DEVICES - 1)

            @pl.when(((k & (PATCHES_Y - 1)) != 0) & (k >= PATCHES_Y))
            def _():
                send_fields(me ^ k, part)

            return carry

        lax.fori_loop(1, DEVICES, send, 0)

    pl.semaphore_wait(barrier, MATES)

    def tell(i, carry):
        pl.semaphore_signal(ready, inc=1, device_id=device(me ^ i), device_id_type=MESH)
        return carry

    lax.fori_loop(1, PATCHES_Y, tell, 0)
    send_mates(0)
    pl.semaphore_wait(ready, PATCHES_Y - 1)
    send_others(0)
    for load in small:
        load.wait()

    def extract(p, carry):
        col = col_ref[pl.ds(p, 1), :] - p * COLS
        var = var_ref[pl.ds(p, 1), :]
        hot = jnp.where(iota((COLS, SLOTS), 0) == col, 1.0, 0.0).astype(bf16)
        tile = xv[:, :, columns_of(p)].reshape(FIELDS * LOCAL, COLS)
        picks = dot(tile, hot, ((1,), (0,)))
        found = jnp.zeros((LOCAL, SLOTS), f32)
        for f in range(FIELDS):
            found = jnp.where(var == f, picks[f * LOCAL : (f + 1) * LOCAL, :], found)
        rows_out[p + 1] = found.astype(bf16)
        return carry

    share = DEVICES // LOAD_PARTS
    for part in range(LOAD_PARTS):
        loads[part].wait()
        lax.fori_loop(part * share, (part + 1) * share, extract, 0, unroll=2)
    rows_out[0] = rows_out[DEVICES]
    rows_out[DEVICES + 1] = rows_out[1]
    rows_in[:, me] = rows_out[pl.ds(me, 3)]
    fields_in[:, me] = xv[:, :, columns_of(me)]

    def send_rows(i, carry):
        t = partner(i)
        pltpu.make_async_remote_copy(
            src_ref=rows_out.at[pl.ds(t, 3)],
            dst_ref=rows_in.at[:, me],
            send_sem=rows_send,
            recv_sem=rows_recv,
            device_id=device(t),
            device_id_type=MESH,
        ).start()
        return carry

    lax.fori_loop(1, DEVICES, send_rows, 0)
    send_mates(1)
    send_others(1)

    window = [lax.rem(me + DEVICES - 1 + w, DEVICES) for w in range(3)]
    lane = iota((1, SLOTS), 1)
    eye = iota((SLOTS, SLOTS), 0) == iota((SLOTS, SLOTS), 1)

    def window_row(ref):
        return jnp.concatenate([ref[pl.ds(q, 1), :] for q in window], axis=1)

    def as_column(row):
        return jnp.sum(jnp.where(eye, row, 0.0), axis=1, keepdims=True)

    present = jnp.concatenate(
        [jnp.where(lane < count_ref[q], 1.0, 0.0).astype(f32) for q in window], axis=1
    )
    values = window_row(value_ref)
    table = jnp.concatenate(
        [
            window_row(err_ref),
            window_row(col_ref).astype(f32),
            present,
            jnp.zeros((5, WINDOW), f32),
        ],
        axis=0,
    )
    for g in range(GROUPS):
        listed = list_ref[g : g + 1, :]
        hot = jnp.where(iota((WINDOW, SLOTS), 0) == listed, 1.0, 0.0).astype(f32)
        onehot[:, g * SLOTS : (g + 1) * SLOTS] = hot.astype(bf16)
        looked = dot(table, hot, ((1,), (0,)), highest)
        err, col, there = looked[0:1, :], looked[1:2, :], looked[2:3, :]
        centre = (me * COLS + g * GROUP_COLS).astype(f32) + 0.5 * (GROUP_COLS - 1)
        offset = col - centre
        total = float(DEVICES * COLS)
        offset = offset - total * jnp.floor(offset / total + 0.5)
        live = (lane < list_count_ref[g]) & (there > 0.5)
        weight = jnp.where(live, jnp.exp(-((offset / COLS) ** 2)) / err, 0.0)
        weight_row[g : g + 1, :] = weight
        weight_col[g] = jnp.broadcast_to(as_column(weight), (SLOTS, SLOTS))

    everyone = rows_in.at[:, pl.ds(0, DEVICES - 1)]
    pltpu.make_async_copy(everyone, everyone, rows_recv).wait()
    means = []
    for w in range(3):
        rows = rows_in[w].reshape(MEMBERS, SLOTS).astype(f32)
        mean = jnp.sum(rows, axis=0, keepdims=True) * (1.0 / MEMBERS)
        means.append(mean)
        pert[:, w * SLOTS : (w + 1) * SLOTS] = (rows - mean).astype(bf16)
    innov = values - jnp.concatenate(means, axis=1)
    innov8 = jnp.concatenate([innov, jnp.zeros((7, WINDOW), f32)], axis=0)
    for g in range(GROUPS):
        span = slice(g * SLOTS, (g + 1) * SLOTS)
        hot = onehot[:, span]
        chosen = dot(pert[...], hot, ((1,), (0,)))
        picked[:, span] = chosen.astype(bf16)
        picked_t[span, :] = jnp.transpose(chosen).astype(bf16)

    identity = jnp.where(eye, 1.0, 0.0).astype(f32)
    for g in range(GROUPS):
        span = slice(g * SLOTS, (g + 1) * SLOTS)
        gram = dot(picked_t[span, :], picked[:, span], ((1,), (0,)))
        bmat = identity + weight_col[g] * gram * weight_row[g : g + 1, :] / dof
        system[g] = bmat
    ymats, zmats, scales = [], [], []
    for g in range(GROUPS):
        bmat = system[g]
        sums = jnp.sum(jnp.abs(bmat), axis=1, keepdims=True)
        scale = jnp.max(sums, axis=0, keepdims=True)
        scales.append(scale)
        ymats.append(bmat / scale)
        zmats.append(None)
    for step in range(NS_STEPS):
        if step == 0:
            tmats = [0.5 * (3.0 * identity - y) for y in ymats]
        else:
            tmats = [
                0.5 * (3.0 * identity - dot(z, y, ((1,), (0,)), highest))
                for z, y in zip(zmats, ymats)
            ]
        ymats = [dot(y, t, ((1,), (0,)), highest) for y, t in zip(ymats, tmats)]
        if step == 0:
            zmats = tmats
        elif step < NS_STEPS - 1:
            zmats = [dot(t, z, ((1,), (0,)), highest) for t, z in zip(tmats, zmats)]
    for g in range(GROUPS):
        system[GROUPS + g] = system[g] + jnp.sqrt(scales[g]) * ymats[g]

    panel_lane = iota((1, SLOTS), 1)
    panel_row = iota((PANEL, SLOTS), 0)
    lanes = iota((SLOTS, SLOTS), 1)

    def thirds(a):
        high = a.astype(bf16)
        rest = a - high.astype(f32)
        mid = rest.astype(bf16)
        return high, mid, (rest - mid.astype(f32)).astype(bf16)

    for b in range(SLOTS // PANEL):
        rows = slice(b * PANEL, (b + 1) * PANEL)
        before = [system[j, rows, :] for j in range(2 * GROUPS)]
        after = list(before)
        for i in range(PANEL):
            c = b * PANEL + i
            here = panel_lane == c
            for j in range(2 * GROUPS):
                now = after[j]
                column = jnp.broadcast_to(now[:, c : c + 1], (PANEL, SLOTS))
                inverse = 1.0 / column[i : i + 1, :]
                scaled = jnp.where(here, -inverse, now[i : i + 1, :] * inverse)
                swept = jnp.where(here, 0.0, now) - column * scaled
                after[j] = jnp.where(panel_row == i, scaled, swept)
        inside = (lanes >= b * PANEL) & (lanes < (b + 1) * PANEL)
        for j in range(2 * GROUPS):
            h, m, l = thirds(before[j])
            p, q, r = thirds(after[j])
            left = jnp.concatenate([h, h, h, m, m, l], axis=0)
            right = jnp.concatenate([p, q, r, p, q, p], axis=0)
            step = dot(left, right, ((0,), (0,)))
            system[j] = jnp.where(inside, 0.0, system[j]) - step
            system[j, rows, :] = after[j]

    group_of = iota((SLOTS, COLS), 1) // GROUP_COLS
    shift_sel = jnp.zeros((SLOTS, COLS), f32)
    for g in range(GROUPS):
        span = slice(g * SLOTS, (g + 1) * SLOTS)
        hot = onehot[:, span].astype(f32)
        seen = dot(innov8, hot, ((1,), (0,)), highest)[0:1, :]
        row = weight_row[g : g + 1, :]
        solved = -jnp.sum(system[g] * (row * seen), axis=1, keepdims=True)
        shift_sel = jnp.where(group_of == g, weight_col[g] * solved / dof, shift_sel)
        mix = weight_col[g] * system[GROUPS + g] * row / dof
        high = mix.astype(bf16)
        low = (mix - high.astype(f32)).astype(bf16)
        mix3[span, 0:SLOTS] = high
        mix3[span, SLOTS : 2 * SLOTS] = high
        mix3[span, 2 * SLOTS : 3 * SLOTS] = low
    shift[...] = shift_sel

    early_in = fields_in.at[pl.ds(0, EARLY), pl.ds(0, DEVICES - 1)]
    late_in = fields_in.at[pl.ds(EARLY, FIELDS - EARLY), pl.ds(0, DEVICES - 1)]
    pltpu.make_async_copy(early_in, early_in, fields_recv.at[0]).wait()

    def update(c, carry):
        first = c * PAIR
        chunk = pl.ds(first, PAIR)

        @pl.when(c == EARLY // PAIR)
        def _():
            pltpu.make_async_copy(late_in, late_in, fields_recv.at[1]).wait()

        whole = [
            fields_in[first + j].reshape(MEMBERS, COLS).astype(f32) for j in range(PAIR)
        ]
        whole = jnp.concatenate(whole, axis=1)
        mean = jnp.sum(whole, axis=0, keepdims=True) * (1.0 / MEMBERS)
        field_pert = (whole - mean).astype(bf16)
        proj = dot(picked_t[...], field_pert, ((1,), (0,)))
        group = (iota((SLOTS, PAIR * COLS), 1) % COLS) // GROUP_COLS
        own = jnp.zeros((SLOTS, PAIR * COLS), f32)
        for g in range(GROUPS):
            own = jnp.where(group == g, proj[g * SLOTS : (g + 1) * SLOTS, :], own)
        both = jnp.concatenate([shift[...]] * PAIR, axis=1)
        mean_term = jnp.sum(both * own, axis=0, keepdims=True)
        high = own.astype(bf16)
        low = (own - high.astype(f32)).astype(bf16)
        split = jnp.concatenate([high, low, high], axis=0)
        spread = dot(mix3[...], split, ((1,), (0,)))
        spread = jnp.concatenate(
            [
                jnp.where(group == g, spread[g * SLOTS : (g + 1) * SLOTS, :], 0.0)
                for g in range(GROUPS)
            ],
            axis=0,
        ).astype(bf16)
        total = whole + mean_term + dot(picked[...], spread, ((1,), (0,)))
        for j in range(PAIR):
            part = total[:, j * COLS : (j + 1) * COLS].astype(bf16)
            fields_out[first + j] = part.reshape(DEVICES, LOCAL, COLS)

        def send_back(i, inner):
            t = partner(i)
            pltpu.make_async_remote_copy(
                src_ref=fields_out.at[chunk, t],
                dst_ref=y_ref.at[chunk, :, columns_of(me)],
                send_sem=back_send,
                recv_sem=back_recv,
                device_id=device(t),
                device_id_type=MESH,
            ).start()
            return inner

        lax.fori_loop(1, DEVICES, send_back, 0)
        return carry

    lax.fori_loop(0, FIELDS // PAIR, update, 0)
    mine = pltpu.make_async_copy(fields_out.at[:, me], y_ref.at[:, :, columns_of(me)], own_sem)
    mine.start()
    sent_rows = rows_in.at[:, pl.ds(0, DEVICES - 1)]
    pltpu.make_async_copy(sent_rows, sent_rows, rows_send).wait()
    pltpu.make_async_copy(early_in, early_in, fields_send.at[0]).wait()
    pltpu.make_async_copy(late_in, late_in, fields_send.at[1]).wait()
    everyone_out = fields_out.at[:, pl.ds(0, DEVICES - 1)]
    pltpu.make_async_copy(everyone_out, everyone_out, back_send).wait()
    pltpu.make_async_copy(everyone_out, everyone_out, back_recv).wait()
    mine.wait()


def shards(ensemble, obs_col, obs_var, obs_value, obs_err, obs_count, coarse_list, coarse_count):
    f32, bf16 = jnp.float32, jnp.bfloat16
    by_field = jnp.transpose(ensemble, (1, 0, 2))
    square = (DEVICES, SLOTS)
    anywhere = pl.BlockSpec(memory_space=pl.ANY)
    blocks = (FIELDS, DEVICES, LOCAL, COLS)
    result = pl.pallas_call(
        kernel,
        out_shape=jax.ShapeDtypeStruct((FIELDS, LOCAL, DEVICES * COLS), bf16),
        in_specs=[anywhere] * 8,
        out_specs=anywhere,
        scratch_shapes=[
            pltpu.VMEM(square, jnp.int32),
            pltpu.VMEM(square, jnp.int32),
            pltpu.VMEM(square, f32),
            pltpu.VMEM(square, f32),
            pltpu.SMEM((DEVICES,), jnp.int32),
            pltpu.VMEM((GROUPS, SLOTS), jnp.int32),
            pltpu.SMEM((GROUPS,), jnp.int32),
            pltpu.SemaphoreType.DMA((7,)),
            pltpu.VMEM((FIELDS, LOCAL, DEVICES * COLS), bf16),
            pltpu.VMEM((DEVICES + 2, LOCAL, SLOTS), bf16),
            pltpu.VMEM((3, DEVICES, LOCAL, SLOTS), bf16),
            pltpu.VMEM(blocks, bf16),
            pltpu.VMEM(blocks, bf16),
            pltpu.VMEM((MEMBERS, WINDOW), bf16),
            pltpu.VMEM((MEMBERS, GROUPS * SLOTS), bf16),
            pltpu.VMEM((GROUPS * SLOTS, MEMBERS), bf16),
            pltpu.VMEM((WINDOW, GROUPS * SLOTS), bf16),
            pltpu.VMEM((8, SLOTS), f32),
            pltpu.VMEM((GROUPS, SLOTS, SLOTS), f32),
            pltpu.VMEM((2 * GROUPS, SLOTS, SLOTS), f32),
            pltpu.VMEM((GROUPS * SLOTS, 3 * SLOTS), bf16),
            pltpu.VMEM((SLOTS, COLS), f32),
            pltpu.SemaphoreType.DMA((LOAD_PARTS,)),
        ]
        + [pltpu.SemaphoreType.DMA] * 2
        + [pltpu.SemaphoreType.DMA((2,))] * 2
        + [pltpu.SemaphoreType.DMA] * 3
        + [pltpu.SemaphoreType.REGULAR],
        compiler_params=pltpu.CompilerParams(
            collective_id=0, has_side_effects=True, vmem_limit_bytes=56 * 1024 * 1024
        ),
        cost_estimate=pl.CostEstimate(
            flops=6_000_000_000, bytes_accessed=12_000_000, transcendentals=1024
        ),
        name="letkf",
    )(
        by_field,
        obs_col.reshape(square),
        obs_var.reshape(square),
        obs_value.reshape(square),
        obs_err.reshape(square),
        obs_count,
        coarse_list,
        coarse_count,
    )
    return jnp.transpose(result, (1, 0, 2))


def solution(mesh):
    return jax.shard_map(
        shards,
        mesh=mesh,
        in_specs=(
            P(("mem", "patch"), None, None),
            P(),
            P(),
            P(),
            P(),
            P(),
            P(("mem", "patch"), None),
            P(("mem", "patch")),
        ),
        out_specs=P(("mem", "patch"), None, None),
        check_vma=False,
    )
```

```python
import jax
import jax.numpy as jnp
from jax import lax
from jax.experimental import pallas as pl
from jax.experimental.pallas import tpu as pltpu
from jax.sharding import PartitionSpec as P

MESH = pl.DeviceIdType.MESH
NS_STEPS = 4
DEVICES = 128
PATCHES_Y = 16
SLOTS = 128
GROUPS = 4
GROUP_COLS = 32
COLS = 128
FIELDS = 12
LOCAL = 8
MEMBERS = 1024
WINDOW = 3 * SLOTS
STRIDE = 45
PAIR = 2
LOAD_PARTS = 4
EARLY = 4
MATES = 22
PANEL = 16


def dot(a, b, dims, precision=None):
    return lax.dot_general(
        a, b, (dims, ((), ())), preferred_element_type=jnp.float32, precision=precision
    )


def iota(shape, dim):
    return lax.broadcasted_iota(jnp.int32, shape, dim)


def kernel(
    x_ref,
    col_any,
    var_any,
    value_any,
    err_any,
    count_any,
    list_any,
    list_count_any,
    y_ref,
    col_ref,
    var_ref,
    value_ref,
    err_ref,
    count_ref,
    list_ref,
    list_count_ref,
    small_sem,
    xv,
    rows_out,
    rows_in,
    fields_in,
    fields_out,
    pert,
    picked,
    picked_t,
    onehot,
    weight_row,
    weight_col,
    system,
    mix3,
    shift,
    load_sem,
    rows_send,
    rows_recv,
    fields_send,
    fields_recv,
    back_send,
    back_recv,
    own_sem,
    ready,
):
    f32, bf16 = jnp.float32, jnp.bfloat16
    highest = lax.Precision.HIGHEST
    mem = lax.axis_index("mem")
    patch = lax.axis_index("patch")
    me = mem * PATCHES_Y + patch
    dof = MEMBERS - 1.0

    def device(t):
        return (t >> 4, t & 15)

    def partner(i):
        return me ^ ((i * STRIDE) & (DEVICES - 1))

    def columns_of(t):
        return pl.ds(pl.multiple_of(t * COLS, COLS), COLS)

    barrier = pltpu.get_barrier_semaphore()

    def mate(i):
        return me ^ jnp.where(i < PATCHES_Y, i, (i - PATCHES_Y + 1) * PATCHES_Y)

    def greet(i, carry):
        pl.semaphore_signal(barrier, inc=1, device_id=device(mate(i)), device_id_type=MESH)
        return carry

    lax.fori_loop(1, MATES + 1, greet, 0)

    small = []
    for k, (source, target) in enumerate(
        [
            (col_any, col_ref),
            (var_any, var_ref),
            (value_any, value_ref),
            (err_any, err_ref),
            (count_any, count_ref),
            (list_any, list_ref),
            (list_count_any, list_count_ref),
        ]
    ):
        load = pltpu.make_async_copy(source, target, small_sem.at[k])
        load.start()
        small.append(load)
    width = DEVICES * COLS // LOAD_PARTS
    loads = []
    for part in range(LOAD_PARTS):
        span = pl.ds(part * width, width)
        load = pltpu.make_async_copy(x_ref.at[:, :, span], xv.at[:, :, span], load_sem.at[part])
        load.start()
        loads.append(load)

    def send_fields(t, part):
        span = pl.ds(0, EARLY) if part == 0 else pl.ds(EARLY, FIELDS - EARLY)
        pltpu.make_async_remote_copy(
            src_ref=x_ref.at[span, :, columns_of(t)],
            dst_ref=fields_in.at[span, me],
            send_sem=fields_send.at[part],
            recv_sem=fields_recv.at[part],
            device_id=device(t),
            device_id_type=MESH,
        ).start()

    def send_mates(part):
        def send(i, carry):
            send_fields(me ^ ((i * 7) & (PATCHES_Y - 1)), part)

            @pl.when(i < 8)
            def _():
                send_fields(me ^ (i * PATCHES_Y), part)

            return carry

        lax.fori_loop(1, PATCHES_Y, send, 0)

    def send_others(part):
        def send(i, carry):
            k = (i * STRIDE) & (DEVICES - 1)

            @pl.when(((k & (PATCHES_Y - 1)) != 0) & (k >= PATCHES_Y))
            def _():
                send_fields(me ^ k, part)

            return carry

        lax.fori_loop(1, DEVICES, send, 0)

    pl.semaphore_wait(barrier, MATES)

    def tell(i, carry):
        pl.semaphore_signal(ready, inc=1, device_id=device(me ^ i), device_id_type=MESH)
        return carry

    lax.fori_loop(1, PATCHES_Y, tell, 0)
    send_mates(0)
    pl.semaphore_wait(ready, PATCHES_Y - 1)
    send_others(0)
    for load in small:
        load.wait()

    place = iota((COLS, SLOTS), 0).astype(f32).astype(bf16)
    one, zero = jnp.ones((COLS, SLOTS), bf16), jnp.zeros((COLS, SLOTS), bf16)

    def extract(p, carry):
        col = col_ref[pl.ds(p, 1), :] - p * COLS
        var = var_ref[pl.ds(p, 1), :]
        near = jnp.broadcast_to(col.astype(f32).astype(bf16), (COLS, SLOTS))
        hot = jnp.where(place == near, one, zero)
        tile = xv[:, :, columns_of(p)].reshape(FIELDS * LOCAL, COLS)
        picks = dot(tile, hot, ((1,), (0,)))
        found = jnp.zeros((LOCAL, SLOTS), f32)
        for f in range(FIELDS):
            found = jnp.where(var == f, picks[f * LOCAL : (f + 1) * LOCAL, :], found)
        rows_out[p + 1] = found.astype(bf16)
        return carry

    share = DEVICES // LOAD_PARTS
    for part in range(LOAD_PARTS):
        loads[part].wait()
        lax.fori_loop(part * share, (part + 1) * share, extract, 0, unroll=4)
    rows_out[0] = rows_out[DEVICES]
    rows_out[DEVICES + 1] = rows_out[1]
    rows_in[:, me] = rows_out[pl.ds(me, 3)]
    fields_in[:, me] = xv[:, :, columns_of(me)]

    def send_rows(i, carry):
        t = partner(i)
        pltpu.make_async_remote_copy(
            src_ref=rows_out.at[pl.ds(t, 3)],
            dst_ref=rows_in.at[:, me],
            send_sem=rows_send,
            recv_sem=rows_recv,
            device_id=device(t),
            device_id_type=MESH,
        ).start()
        return carry

    lax.fori_loop(1, DEVICES, send_rows, 0)
    send_mates(1)
    send_others(1)

    window = [lax.rem(me + DEVICES - 1 + w, DEVICES) for w in range(3)]
    lane = iota((1, SLOTS), 1)
    eye = iota((SLOTS, SLOTS), 0) == iota((SLOTS, SLOTS), 1)

    def window_row(ref):
        return jnp.concatenate([ref[pl.ds(q, 1), :] for q in window], axis=1)

    def as_column(row):
        return jnp.sum(jnp.where(eye, row, 0.0), axis=1, keepdims=True)

    present = jnp.concatenate(
        [jnp.where(lane < count_ref[q], 1.0, 0.0).astype(f32) for q in window], axis=1
    )
    values = window_row(value_ref)
    table = jnp.concatenate(
        [
            window_row(err_ref),
            window_row(col_ref).astype(f32),
            present,
            jnp.zeros((5, WINDOW), f32),
        ],
        axis=0,
    )
    for g in range(GROUPS):
        listed = list_ref[g : g + 1, :]
        hot = jnp.where(iota((WINDOW, SLOTS), 0) == listed, 1.0, 0.0).astype(f32)
        onehot[:, g * SLOTS : (g + 1) * SLOTS] = hot.astype(bf16)
        looked = dot(table, hot, ((1,), (0,)), highest)
        err, col, there = looked[0:1, :], looked[1:2, :], looked[2:3, :]
        centre = (me * COLS + g * GROUP_COLS).astype(f32) + 0.5 * (GROUP_COLS - 1)
        offset = col - centre
        total = float(DEVICES * COLS)
        offset = offset - total * jnp.floor(offset / total + 0.5)
        live = (lane < list_count_ref[g]) & (there > 0.5)
        weight = jnp.where(live, jnp.exp(-((offset / COLS) ** 2)) / err, 0.0)
        weight_row[g : g + 1, :] = weight
        weight_col[g] = jnp.broadcast_to(as_column(weight), (SLOTS, SLOTS))

    everyone = rows_in.at[:, pl.ds(0, DEVICES - 1)]
    pltpu.make_async_copy(everyone, everyone, rows_recv).wait()
    means = []
    for w in range(3):
        rows = rows_in[w].reshape(MEMBERS, SLOTS).astype(f32)
        mean = jnp.sum(rows, axis=0, keepdims=True) * (1.0 / MEMBERS)
        means.append(mean)
        pert[:, w * SLOTS : (w + 1) * SLOTS] = (rows - mean).astype(bf16)
    innov = values - jnp.concatenate(means, axis=1)
    innov8 = jnp.concatenate([innov, jnp.zeros((7, WINDOW), f32)], axis=0)
    for g in range(GROUPS):
        span = slice(g * SLOTS, (g + 1) * SLOTS)
        hot = onehot[:, span]
        chosen = dot(pert[...], hot, ((1,), (0,)))
        picked[:, span] = chosen.astype(bf16)
        picked_t[span, :] = jnp.transpose(chosen).astype(bf16)

    identity = jnp.where(eye, 1.0, 0.0).astype(f32)
    for g in range(GROUPS):
        span = slice(g * SLOTS, (g + 1) * SLOTS)
        gram = dot(picked_t[span, :], picked[:, span], ((1,), (0,)))
        bmat = identity + weight_col[g] * gram * weight_row[g : g + 1, :] / dof
        system[g] = bmat
    ymats, zmats, scales = [], [], []
    for g in range(GROUPS):
        bmat = system[g]
        sums = jnp.sum(jnp.abs(bmat), axis=1, keepdims=True)
        scale = jnp.max(sums, axis=0, keepdims=True)
        scales.append(scale)
        ymats.append(bmat / scale)
        zmats.append(None)
    for step in range(NS_STEPS):
        if step == 0:
            tmats = [0.5 * (3.0 * identity - y) for y in ymats]
        else:
            tmats = [
                0.5 * (3.0 * identity - dot(z, y, ((1,), (0,)), highest))
                for z, y in zip(zmats, ymats)
            ]
        ymats = [dot(y, t, ((1,), (0,)), highest) for y, t in zip(ymats, tmats)]
        if step == 0:
            zmats = tmats
        elif step < NS_STEPS - 1:
            zmats = [dot(t, z, ((1,), (0,)), highest) for t, z in zip(tmats, zmats)]
    for g in range(GROUPS):
        system[GROUPS + g] = system[g] + jnp.sqrt(scales[g]) * ymats[g]

    panel_lane = iota((1, SLOTS), 1)
    panel_row = iota((PANEL, SLOTS), 0)
    lanes = iota((SLOTS, SLOTS), 1)

    def thirds(a):
        high = a.astype(bf16)
        rest = a - high.astype(f32)
        mid = rest.astype(bf16)
        return high, mid, (rest - mid.astype(f32)).astype(bf16)

    for b in range(SLOTS // PANEL):
        rows = slice(b * PANEL, (b + 1) * PANEL)
        before = [system[j, rows, :] for j in range(2 * GROUPS)]
        after = list(before)
        for i in range(PANEL):
            c = b * PANEL + i
            here = panel_lane == c
            for j in range(2 * GROUPS):
                now = after[j]
                column = jnp.broadcast_to(now[:, c : c + 1], (PANEL, SLOTS))
                inverse = 1.0 / column[i : i + 1, :]
                scaled = jnp.where(here, -inverse, now[i : i + 1, :] * inverse)
                swept = jnp.where(here, 0.0, now) - column * scaled
                after[j] = jnp.where(panel_row == i, scaled, swept)
        inside = (lanes >= b * PANEL) & (lanes < (b + 1) * PANEL)
        for j in range(2 * GROUPS):
            h, m, l = thirds(before[j])
            p, q, r = thirds(after[j])
            left = jnp.concatenate([h, h, h, m, m, l], axis=0)
            right = jnp.concatenate([p, q, r, p, q, p], axis=0)
            step = dot(left, right, ((0,), (0,)))
            system[j] = jnp.where(inside, 0.0, system[j]) - step
            system[j, rows, :] = after[j]

    group_of = iota((SLOTS, COLS), 1) // GROUP_COLS
    shift_sel = jnp.zeros((SLOTS, COLS), f32)
    for g in range(GROUPS):
        span = slice(g * SLOTS, (g + 1) * SLOTS)
        hot = onehot[:, span].astype(f32)
        seen = dot(innov8, hot, ((1,), (0,)), highest)[0:1, :]
        row = weight_row[g : g + 1, :]
        solved = -jnp.sum(system[g] * (row * seen), axis=1, keepdims=True)
        shift_sel = jnp.where(group_of == g, weight_col[g] * solved / dof, shift_sel)
        mix = weight_col[g] * system[GROUPS + g] * row / dof
        high = mix.astype(bf16)
        low = (mix - high.astype(f32)).astype(bf16)
        mix3[span, 0:SLOTS] = high
        mix3[span, SLOTS : 2 * SLOTS] = high
        mix3[span, 2 * SLOTS : 3 * SLOTS] = low
    shift[...] = shift_sel

    early_in = fields_in.at[pl.ds(0, EARLY), pl.ds(0, DEVICES - 1)]
    late_in = fields_in.at[pl.ds(EARLY, FIELDS - EARLY), pl.ds(0, DEVICES - 1)]
    pltpu.make_async_copy(early_in, early_in, fields_recv.at[0]).wait()

    def update(c, carry):
        first = c * PAIR
        chunk = pl.ds(first, PAIR)

        @pl.when(c == EARLY // PAIR)
        def _():
            pltpu.make_async_copy(late_in, late_in, fields_recv.at[1]).wait()

        whole = [
            fields_in[first + j].reshape(MEMBERS, COLS).astype(f32) for j in range(PAIR)
        ]
        whole = jnp.concatenate(whole, axis=1)
        mean = jnp.sum(whole, axis=0, keepdims=True) * (1.0 / MEMBERS)
        field_pert = (whole - mean).astype(bf16)
        proj = dot(picked_t[...], field_pert, ((1,), (0,)))
        group = (iota((SLOTS, PAIR * COLS), 1) % COLS) // GROUP_COLS
        own = jnp.zeros((SLOTS, PAIR * COLS), f32)
        for g in range(GROUPS):
            own = jnp.where(group == g, proj[g * SLOTS : (g + 1) * SLOTS, :], own)
        both = jnp.concatenate([shift[...]] * PAIR, axis=1)
        mean_term = jnp.sum(both * own, axis=0, keepdims=True)
        high = own.astype(bf16)
        low = (own - high.astype(f32)).astype(bf16)
        split = jnp.concatenate([high, low, high], axis=0)
        spread = dot(mix3[...], split, ((1,), (0,)))
        spread = jnp.concatenate(
            [
                jnp.where(group == g, spread[g * SLOTS : (g + 1) * SLOTS, :], 0.0)
                for g in range(GROUPS)
            ],
            axis=0,
        ).astype(bf16)
        total = whole + mean_term + dot(picked[...], spread, ((1,), (0,)))
        for j in range(PAIR):
            part = total[:, j * COLS : (j + 1) * COLS].astype(bf16)
            fields_out[first + j] = part.reshape(DEVICES, LOCAL, COLS)

        def send_back(i, inner):
            t = partner(i)
            pltpu.make_async_remote_copy(
                src_ref=fields_out.at[chunk, t],
                dst_ref=y_ref.at[chunk, :, columns_of(me)],
                send_sem=back_send,
                recv_sem=back_recv,
                device_id=device(t),
                device_id_type=MESH,
            ).start()
            return inner

        lax.fori_loop(1, DEVICES, send_back, 0)
        return carry

    lax.fori_loop(0, FIELDS // PAIR, update, 0)
    mine = pltpu.make_async_copy(fields_out.at[:, me], y_ref.at[:, :, columns_of(me)], own_sem)
    mine.start()
    sent_rows = rows_in.at[:, pl.ds(0, DEVICES - 1)]
    pltpu.make_async_copy(sent_rows, sent_rows, rows_send).wait()
    pltpu.make_async_copy(early_in, early_in, fields_send.at[0]).wait()
    pltpu.make_async_copy(late_in, late_in, fields_send.at[1]).wait()
    everyone_out = fields_out.at[:, pl.ds(0, DEVICES - 1)]
    pltpu.make_async_copy(everyone_out, everyone_out, back_send).wait()
    pltpu.make_async_copy(everyone_out, everyone_out, back_recv).wait()
    mine.wait()


def shards(ensemble, obs_col, obs_var, obs_value, obs_err, obs_count, coarse_list, coarse_count):
    f32, bf16 = jnp.float32, jnp.bfloat16
    by_field = jnp.transpose(ensemble, (1, 0, 2))
    square = (DEVICES, SLOTS)
    anywhere = pl.BlockSpec(memory_space=pl.ANY)
    blocks = (FIELDS, DEVICES, LOCAL, COLS)
    result = pl.pallas_call(
        kernel,
        out_shape=jax.ShapeDtypeStruct((FIELDS, LOCAL, DEVICES * COLS), bf16),
        in_specs=[anywhere] * 8,
        out_specs=anywhere,
        scratch_shapes=[
            pltpu.VMEM(square, jnp.int32),
            pltpu.VMEM(square, jnp.int32),
            pltpu.VMEM(square, f32),
            pltpu.VMEM(square, f32),
            pltpu.SMEM((DEVICES,), jnp.int32),
            pltpu.VMEM((GROUPS, SLOTS), jnp.int32),
            pltpu.SMEM((GROUPS,), jnp.int32),
            pltpu.SemaphoreType.DMA((7,)),
            pltpu.VMEM((FIELDS, LOCAL, DEVICES * COLS), bf16),
            pltpu.VMEM((DEVICES + 2, LOCAL, SLOTS), bf16),
            pltpu.VMEM((3, DEVICES, LOCAL, SLOTS), bf16),
            pltpu.VMEM(blocks, bf16),
            pltpu.VMEM(blocks, bf16),
            pltpu.VMEM((MEMBERS, WINDOW), bf16),
            pltpu.VMEM((MEMBERS, GROUPS * SLOTS), bf16),
            pltpu.VMEM((GROUPS * SLOTS, MEMBERS), bf16),
            pltpu.VMEM((WINDOW, GROUPS * SLOTS), bf16),
            pltpu.VMEM((8, SLOTS), f32),
            pltpu.VMEM((GROUPS, SLOTS, SLOTS), f32),
            pltpu.VMEM((2 * GROUPS, SLOTS, SLOTS), f32),
            pltpu.VMEM((GROUPS * SLOTS, 3 * SLOTS), bf16),
            pltpu.VMEM((SLOTS, COLS), f32),
            pltpu.SemaphoreType.DMA((LOAD_PARTS,)),
        ]
        + [pltpu.SemaphoreType.DMA] * 2
        + [pltpu.SemaphoreType.DMA((2,))] * 2
        + [pltpu.SemaphoreType.DMA] * 3
        + [pltpu.SemaphoreType.REGULAR],
        compiler_params=pltpu.CompilerParams(
            collective_id=0, has_side_effects=True, vmem_limit_bytes=56 * 1024 * 1024
        ),
        cost_estimate=pl.CostEstimate(
            flops=6_000_000_000, bytes_accessed=12_000_000, transcendentals=1024
        ),
        name="letkf",
    )(
        by_field,
        obs_col.reshape(square),
        obs_var.reshape(square),
        obs_value.reshape(square),
        obs_err.reshape(square),
        obs_count,
        coarse_list,
        coarse_count,
    )
    return jnp.transpose(result, (1, 0, 2))


def solution(mesh):
    return jax.shard_map(
        shards,
        mesh=mesh,
        in_specs=(
            P(("mem", "patch"), None, None),
            P(),
            P(),
            P(),
            P(),
            P(),
            P(("mem", "patch"), None),
            P(("mem", "patch")),
        ),
        out_specs=P(("mem", "patch"), None, None),
        check_vma=False,
    )
```

```python
import jax
import jax.numpy as jnp
from jax import lax
from jax.experimental import pallas as pl
from jax.experimental.pallas import tpu as pltpu
from jax.sharding import PartitionSpec as P

MESH = pl.DeviceIdType.MESH
NS_STEPS = 4
DEVICES = 128
PATCHES_Y = 16
SLOTS = 128
GROUPS = 4
GROUP_COLS = 32
COLS = 128
FIELDS = 12
LOCAL = 8
MEMBERS = 1024
WINDOW = 3 * SLOTS
STRIDE = 45
PAIR = 2
LOAD_PARTS = 4
EARLY = 4
MATES = 22
PANEL = 16


def dot(a, b, dims, precision=None):
    return lax.dot_general(
        a, b, (dims, ((), ())), preferred_element_type=jnp.float32, precision=precision
    )


def iota(shape, dim):
    return lax.broadcasted_iota(jnp.int32, shape, dim)


def kernel(
    x_ref,
    col_any,
    var_any,
    value_any,
    err_any,
    count_any,
    list_any,
    list_count_any,
    y_ref,
    col_ref,
    var_ref,
    value_ref,
    err_ref,
    count_ref,
    list_ref,
    list_count_ref,
    small_sem,
    xv,
    rows_out,
    rows_in,
    fields_in,
    fields_out,
    pert,
    picked,
    picked_t,
    onehot,
    weight_row,
    weight_col,
    system,
    mix3,
    shift,
    load_sem,
    rows_send,
    rows_recv,
    fields_send,
    fields_recv,
    back_send,
    back_recv,
    own_sem,
    ready,
):
    f32, bf16 = jnp.float32, jnp.bfloat16
    highest = lax.Precision.HIGHEST
    mem = lax.axis_index("mem")
    patch = lax.axis_index("patch")
    me = mem * PATCHES_Y + patch
    dof = MEMBERS - 1.0

    def device(t):
        return (t >> 4, t & 15)

    def partner(i):
        return me ^ ((i * STRIDE) & (DEVICES - 1))

    def columns_of(t):
        return pl.ds(pl.multiple_of(t * COLS, COLS), COLS)

    barrier = pltpu.get_barrier_semaphore()

    def mate(i):
        return me ^ jnp.where(i < PATCHES_Y, i, (i - PATCHES_Y + 1) * PATCHES_Y)

    def greet(i, carry):
        pl.semaphore_signal(barrier, inc=1, device_id=device(mate(i)), device_id_type=MESH)
        return carry

    lax.fori_loop(1, MATES + 1, greet, 0)

    small = []
    for k, (source, target) in enumerate(
        [
            (col_any, col_ref),
            (var_any, var_ref),
            (value_any, value_ref),
            (err_any, err_ref),
            (count_any, count_ref),
            (list_any, list_ref),
            (list_count_any, list_count_ref),
        ]
    ):
        load = pltpu.make_async_copy(source, target, small_sem.at[k])
        load.start()
        small.append(load)
    width = DEVICES * COLS // LOAD_PARTS
    loads = []
    for part in range(LOAD_PARTS):
        span = pl.ds(part * width, width)
        load = pltpu.make_async_copy(x_ref.at[:, :, span], xv.at[:, :, span], load_sem.at[part])
        load.start()
        loads.append(load)

    def send_fields(t, part):
        span = pl.ds(0, EARLY) if part == 0 else pl.ds(EARLY, FIELDS - EARLY)
        pltpu.make_async_remote_copy(
            src_ref=x_ref.at[span, :, columns_of(t)],
            dst_ref=fields_in.at[span, me],
            send_sem=fields_send.at[part],
            recv_sem=fields_recv.at[part],
            device_id=device(t),
            device_id_type=MESH,
        ).start()

    def send_mates(part):
        def send(i, carry):
            send_fields(me ^ ((i * 7) & (PATCHES_Y - 1)), part)

            @pl.when(i < 8)
            def _():
                send_fields(me ^ (i * PATCHES_Y), part)

            return carry

        lax.fori_loop(1, PATCHES_Y, send, 0)

    def send_others(part):
        def send(i, carry):
            k = (i * STRIDE) & (DEVICES - 1)

            @pl.when(((k & (PATCHES_Y - 1)) != 0) & (k >= PATCHES_Y))
            def _():
                send_fields(me ^ k, part)

            return carry

        lax.fori_loop(1, DEVICES, send, 0)

    pl.semaphore_wait(barrier, MATES)

    def tell(i, carry):
        pl.semaphore_signal(ready, inc=1, device_id=device(me ^ i), device_id_type=MESH)
        return carry

    lax.fori_loop(1, PATCHES_Y, tell, 0)
    send_mates(0)
    pl.semaphore_wait(ready, PATCHES_Y - 1)
    send_others(0)
    for load in small:
        load.wait()

    place = iota((COLS, SLOTS), 0).astype(f32).astype(bf16)
    one, zero = jnp.ones((COLS, SLOTS), bf16), jnp.zeros((COLS, SLOTS), bf16)

    def extract(p, carry):
        col = col_ref[pl.ds(p, 1), :] - p * COLS
        var = var_ref[pl.ds(p, 1), :]
        near = jnp.broadcast_to(col.astype(f32).astype(bf16), (COLS, SLOTS))
        hot = jnp.where(place == near, one, zero)
        tile = xv[:, :, columns_of(p)].reshape(FIELDS * LOCAL, COLS)
        picks = dot(tile, hot, ((1,), (0,)))
        found = jnp.zeros((LOCAL, SLOTS), f32)
        for f in range(FIELDS):
            found = jnp.where(var == f, picks[f * LOCAL : (f + 1) * LOCAL, :], found)
        rows_out[p + 1] = found.astype(bf16)
        return carry

    share = DEVICES // LOAD_PARTS
    for part in range(LOAD_PARTS):
        loads[part].wait()
        lax.fori_loop(part * share, (part + 1) * share, extract, 0, unroll=4)
    rows_out[0] = rows_out[DEVICES]
    rows_out[DEVICES + 1] = rows_out[1]
    rows_in[:, me] = rows_out[pl.ds(me, 3)]
    fields_in[:, me] = xv[:, :, columns_of(me)]

    def send_rows(i, carry):
        t = partner(i)
        pltpu.make_async_remote_copy(
            src_ref=rows_out.at[pl.ds(t, 3)],
            dst_ref=rows_in.at[:, me],
            send_sem=rows_send,
            recv_sem=rows_recv,
            device_id=device(t),
            device_id_type=MESH,
        ).start()
        return carry

    lax.fori_loop(1, DEVICES, send_rows, 0)
    send_mates(1)
    send_others(1)

    window = [lax.rem(me + DEVICES - 1 + w, DEVICES) for w in range(3)]
    lane = iota((1, SLOTS), 1)
    eye = iota((SLOTS, SLOTS), 0) == iota((SLOTS, SLOTS), 1)

    def window_row(ref):
        return jnp.concatenate([ref[pl.ds(q, 1), :] for q in window], axis=1)

    def as_column(row):
        return jnp.sum(jnp.where(eye, row, 0.0), axis=1, keepdims=True)

    present = jnp.concatenate(
        [jnp.where(lane < count_ref[q], 1.0, 0.0).astype(f32) for q in window], axis=1
    )
    values = window_row(value_ref)
    table = jnp.concatenate(
        [
            window_row(err_ref),
            window_row(col_ref).astype(f32),
            present,
            jnp.zeros((5, WINDOW), f32),
        ],
        axis=0,
    )
    for g in range(GROUPS):
        listed = list_ref[g : g + 1, :]
        hot = jnp.where(iota((WINDOW, SLOTS), 0) == listed, 1.0, 0.0).astype(f32)
        onehot[:, g * SLOTS : (g + 1) * SLOTS] = hot.astype(bf16)
        looked = dot(table, hot, ((1,), (0,)), highest)
        err, col, there = looked[0:1, :], looked[1:2, :], looked[2:3, :]
        centre = (me * COLS + g * GROUP_COLS).astype(f32) + 0.5 * (GROUP_COLS - 1)
        offset = col - centre
        total = float(DEVICES * COLS)
        offset = offset - total * jnp.floor(offset / total + 0.5)
        live = (lane < list_count_ref[g]) & (there > 0.5)
        weight = jnp.where(live, jnp.exp(-((offset / COLS) ** 2)) / err, 0.0)
        weight_row[g : g + 1, :] = weight
        weight_col[g] = jnp.broadcast_to(as_column(weight), (SLOTS, SLOTS))

    everyone = rows_in.at[:, pl.ds(0, DEVICES - 1)]
    pltpu.make_async_copy(everyone, everyone, rows_recv).wait()
    means = []
    for w in range(3):
        rows = rows_in[w].reshape(MEMBERS, SLOTS).astype(f32)
        mean = jnp.sum(rows, axis=0, keepdims=True) * (1.0 / MEMBERS)
        means.append(mean)
        pert[:, w * SLOTS : (w + 1) * SLOTS] = (rows - mean).astype(bf16)
    innov = values - jnp.concatenate(means, axis=1)
    innov8 = jnp.concatenate([innov, jnp.zeros((7, WINDOW), f32)], axis=0)
    for g in range(GROUPS):
        span = slice(g * SLOTS, (g + 1) * SLOTS)
        hot = onehot[:, span]
        chosen = dot(pert[...], hot, ((1,), (0,)))
        picked[:, span] = chosen.astype(bf16)
        picked_t[span, :] = jnp.transpose(chosen).astype(bf16)

    identity = jnp.where(eye, 1.0, 0.0).astype(f32)
    for g in range(GROUPS):
        span = slice(g * SLOTS, (g + 1) * SLOTS)
        gram = dot(picked_t[span, :], picked[:, span], ((1,), (0,)))
        bmat = identity + weight_col[g] * gram * weight_row[g : g + 1, :] / dof
        system[g] = bmat
    ymats, zmats, scales = [], [], []
    for g in range(GROUPS):
        bmat = system[g]
        sums = jnp.sum(jnp.abs(bmat), axis=1, keepdims=True)
        scale = jnp.max(sums, axis=0, keepdims=True)
        scales.append(scale)
        ymats.append(bmat / scale)
        zmats.append(None)
    for step in range(NS_STEPS):
        if step == 0:
            tmats = [0.5 * (3.0 * identity - y) for y in ymats]
        else:
            tmats = [
                0.5 * (3.0 * identity - dot(z, y, ((1,), (0,)), highest))
                for z, y in zip(zmats, ymats)
            ]
        ymats = [dot(y, t, ((1,), (0,)), highest) for y, t in zip(ymats, tmats)]
        if step == 0:
            zmats = tmats
        elif step < NS_STEPS - 1:
            zmats = [dot(t, z, ((1,), (0,)), highest) for t, z in zip(tmats, zmats)]
    for g in range(GROUPS):
        system[GROUPS + g] = system[g] + jnp.sqrt(scales[g]) * ymats[g]

    panel_lane = iota((1, SLOTS), 1)
    panel_row = iota((PANEL, SLOTS), 0)
    lanes = iota((SLOTS, SLOTS), 1)

    def thirds(a):
        high = a.astype(bf16)
        rest = a - high.astype(f32)
        mid = rest.astype(bf16)
        return high, mid, (rest - mid.astype(f32)).astype(bf16)

    for b in range(SLOTS // PANEL):
        rows = slice(b * PANEL, (b + 1) * PANEL)
        before = [system[j, rows, :] for j in range(2 * GROUPS)]
        after = list(before)
        for i in range(PANEL):
            c = b * PANEL + i
            here = panel_lane == c
            for j in range(2 * GROUPS):
                now = after[j]
                column = jnp.broadcast_to(now[:, c : c + 1], (PANEL, SLOTS))
                inverse = 1.0 / column[i : i + 1, :]
                scaled = jnp.where(here, -inverse, now[i : i + 1, :] * inverse)
                swept = jnp.where(here, 0.0, now) - column * scaled
                after[j] = jnp.where(panel_row == i, scaled, swept)
        inside = (lanes >= b * PANEL) & (lanes < (b + 1) * PANEL)
        for j in range(2 * GROUPS):
            h, m, l = thirds(before[j])
            p, q, r = thirds(after[j])
            left = jnp.concatenate([h, h, h, m, m, l], axis=0)
            right = jnp.concatenate([p, q, r, p, q, p], axis=0)
            step = dot(left, right, ((0,), (0,)))
            system[j] = jnp.where(inside, 0.0, system[j]) - step
            system[j, rows, :] = after[j]

    group_of = iota((SLOTS, COLS), 1) // GROUP_COLS
    shift_sel = jnp.zeros((SLOTS, COLS), f32)
    for g in range(GROUPS):
        span = slice(g * SLOTS, (g + 1) * SLOTS)
        hot = onehot[:, span].astype(f32)
        seen = dot(innov8, hot, ((1,), (0,)), highest)[0:1, :]
        row = weight_row[g : g + 1, :]
        solved = -jnp.sum(system[g] * (row * seen), axis=1, keepdims=True)
        shift_sel = jnp.where(group_of == g, weight_col[g] * solved / dof, shift_sel)
        mix = weight_col[g] * system[GROUPS + g] * row / dof
        high = mix.astype(bf16)
        low = (mix - high.astype(f32)).astype(bf16)
        mix3[span, 0:SLOTS] = high
        mix3[span, SLOTS : 2 * SLOTS] = high
        mix3[span, 2 * SLOTS : 3 * SLOTS] = low
    shift[...] = shift_sel

    early_in = fields_in.at[pl.ds(0, EARLY), pl.ds(0, DEVICES - 1)]
    late_in = fields_in.at[pl.ds(EARLY, FIELDS - EARLY), pl.ds(0, DEVICES - 1)]
    pltpu.make_async_copy(early_in, early_in, fields_recv.at[0]).wait()

    def update(c, carry):
        first = c * PAIR
        chunk = pl.ds(first, PAIR)

        @pl.when(c == EARLY // PAIR)
        def _():
            pltpu.make_async_copy(late_in, late_in, fields_recv.at[1]).wait()

        whole = [
            fields_in[first + j].reshape(MEMBERS, COLS).astype(f32) for j in range(PAIR)
        ]
        whole = jnp.concatenate(whole, axis=1)
        mean = jnp.sum(whole, axis=0, keepdims=True) * (1.0 / MEMBERS)
        field_pert = (whole - mean).astype(bf16)
        proj = dot(picked_t[...], field_pert, ((1,), (0,)))
        group = (iota((SLOTS, PAIR * COLS), 1) % COLS) // GROUP_COLS
        own = jnp.zeros((SLOTS, PAIR * COLS), f32)
        for g in range(GROUPS):
            own = jnp.where(group == g, proj[g * SLOTS : (g + 1) * SLOTS, :], own)
        both = jnp.concatenate([shift[...]] * PAIR, axis=1)
        mean_term = jnp.sum(both * own, axis=0, keepdims=True)
        high = own.astype(bf16)
        low = (own - high.astype(f32)).astype(bf16)
        split = jnp.concatenate([high, low, high], axis=0)
        spread = dot(mix3[...], split, ((1,), (0,)))
        spread = jnp.concatenate(
            [
                jnp.where(group == g, spread[g * SLOTS : (g + 1) * SLOTS, :], 0.0)
                for g in range(GROUPS)
            ],
            axis=0,
        ).astype(bf16)
        total = whole + mean_term + dot(picked[...], spread, ((1,), (0,)))
        for j in range(PAIR):
            part = total[:, j * COLS : (j + 1) * COLS].astype(bf16)
            fields_out[first + j] = part.reshape(DEVICES, LOCAL, COLS)

        def send_back(i):
            t = partner(i)
            pltpu.make_async_remote_copy(
                src_ref=fields_out.at[chunk, t],
                dst_ref=y_ref.at[chunk, :, columns_of(me)],
                send_sem=back_send,
                recv_sem=back_recv,
                device_id=device(t),
                device_id_type=MESH,
            ).start()

        def send_four(i, inner):
            for j in range(4):
                send_back(4 * i + j)
            return inner

        for i in range(1, 4):
            send_back(i)
        lax.fori_loop(1, DEVICES // 4, send_four, 0)
        return carry

    lax.fori_loop(0, FIELDS // PAIR, update, 0)
    mine = pltpu.make_async_copy(fields_out.at[:, me], y_ref.at[:, :, columns_of(me)], own_sem)
    mine.start()
    sent_rows = rows_in.at[:, pl.ds(0, DEVICES - 1)]
    pltpu.make_async_copy(sent_rows, sent_rows, rows_send).wait()
    pltpu.make_async_copy(early_in, early_in, fields_send.at[0]).wait()
    pltpu.make_async_copy(late_in, late_in, fields_send.at[1]).wait()
    everyone_out = fields_out.at[:, pl.ds(0, DEVICES - 1)]
    pltpu.make_async_copy(everyone_out, everyone_out, back_send).wait()
    pltpu.make_async_copy(everyone_out, everyone_out, back_recv).wait()
    mine.wait()


def shards(ensemble, obs_col, obs_var, obs_value, obs_err, obs_count, coarse_list, coarse_count):
    f32, bf16 = jnp.float32, jnp.bfloat16
    by_field = jnp.transpose(ensemble, (1, 0, 2))
    square = (DEVICES, SLOTS)
    anywhere = pl.BlockSpec(memory_space=pl.ANY)
    blocks = (FIELDS, DEVICES, LOCAL, COLS)
    result = pl.pallas_call(
        kernel,
        out_shape=jax.ShapeDtypeStruct((FIELDS, LOCAL, DEVICES * COLS), bf16),
        in_specs=[anywhere] * 8,
        out_specs=anywhere,
        scratch_shapes=[
            pltpu.VMEM(square, jnp.int32),
            pltpu.VMEM(square, jnp.int32),
            pltpu.VMEM(square, f32),
            pltpu.VMEM(square, f32),
            pltpu.SMEM((DEVICES,), jnp.int32),
            pltpu.VMEM((GROUPS, SLOTS), jnp.int32),
            pltpu.SMEM((GROUPS,), jnp.int32),
            pltpu.SemaphoreType.DMA((7,)),
            pltpu.VMEM((FIELDS, LOCAL, DEVICES * COLS), bf16),
            pltpu.VMEM((DEVICES + 2, LOCAL, SLOTS), bf16),
            pltpu.VMEM((3, DEVICES, LOCAL, SLOTS), bf16),
            pltpu.VMEM(blocks, bf16),
            pltpu.VMEM(blocks, bf16),
            pltpu.VMEM((MEMBERS, WINDOW), bf16),
            pltpu.VMEM((MEMBERS, GROUPS * SLOTS), bf16),
            pltpu.VMEM((GROUPS * SLOTS, MEMBERS), bf16),
            pltpu.VMEM((WINDOW, GROUPS * SLOTS), bf16),
            pltpu.VMEM((8, SLOTS), f32),
            pltpu.VMEM((GROUPS, SLOTS, SLOTS), f32),
            pltpu.VMEM((2 * GROUPS, SLOTS, SLOTS), f32),
            pltpu.VMEM((GROUPS * SLOTS, 3 * SLOTS), bf16),
            pltpu.VMEM((SLOTS, COLS), f32),
            pltpu.SemaphoreType.DMA((LOAD_PARTS,)),
        ]
        + [pltpu.SemaphoreType.DMA] * 2
        + [pltpu.SemaphoreType.DMA((2,))] * 2
        + [pltpu.SemaphoreType.DMA] * 3
        + [pltpu.SemaphoreType.REGULAR],
        compiler_params=pltpu.CompilerParams(
            collective_id=0, has_side_effects=True, vmem_limit_bytes=56 * 1024 * 1024
        ),
        cost_estimate=pl.CostEstimate(
            flops=6_000_000_000, bytes_accessed=12_000_000, transcendentals=1024
        ),
        name="letkf",
    )(
        by_field,
        obs_col.reshape(square),
        obs_var.reshape(square),
        obs_value.reshape(square),
        obs_err.reshape(square),
        obs_count,
        coarse_list,
        coarse_count,
    )
    return jnp.transpose(result, (1, 0, 2))


def solution(mesh):
    return jax.shard_map(
        shards,
        mesh=mesh,
        in_specs=(
            P(("mem", "patch"), None, None),
            P(),
            P(),
            P(),
            P(),
            P(),
            P(("mem", "patch"), None),
            P(("mem", "patch")),
        ),
        out_specs=P(("mem", "patch"), None, None),
        check_vma=False,
    )
```
